32 devices in a mesh: parts: 2 (over x), region: 2 (over core), shard: 8 (over z, y).
Axes of the slice: x: 2, y: 2, z: 4, core: 2. Of those that a mesh axis runs over, the one named last changes fastest.
Arguments:
- vectors: bfloat16 [131072, 768], P(('parts', 'region', 'shard')), parts along dimension 0, may hold values from -6 to 6
- tile_region: int32 [1024], P(('parts', 'region', 'shard')), parts along dimension 0, may hold values from 0 to 1, as said below
- tile_block: int32 [1024], P(('parts', 'region', 'shard')), parts along dimension 0, may hold values from 0 to 63
- primary_pick: int32 [131072], P(('parts', 'region', 'shard')), parts along dimension 0, may hold values from 0 to 511
- spill_pick: int32 [131072], P(('parts', 'region', 'shard')), parts along dimension 0, may hold values from 0 to 511
- centers: bfloat16 [2, 32768, 768], P('region', 'shard'), may hold values from -6 to 6
Outputs:
- spill_scores: bfloat16 [131072, 512], P(('parts', 'region', 'shard')), parts along dimension 0
- primary_score: bfloat16 [131072], P(('parts', 'region', 'shard')), parts along dimension 0
- spill_chosen: bfloat16 [131072], P(('parts', 'region', 'shard')), parts along dimension 0
The draws below stay inside these ranges and needn't reach their ends.
There are 2 independent parts, one for each index of `parts`. The reference program is written for one: setup_inputs(seed, part) draws one part's arguments, and reference() takes and returns one part's arrays. A program takes and returns all parts, laid end to end along the dimension named above; an argument that names none is the same for every part. Nothing has to cross between parts.
Inputs may be any that keep to these rules, and one draw needn't show every extreme that they name: For the 64 tiles of one device (aligned blocks of tile_region and tile_block), the pair (tile_region, tile_block // 8) takes any one value at most 4 times, and some value exactly 4 times.
All inputs are finite; a program needn't handle non-finite values.
Results may differ from the reference program's by a relative error of at most 0.0034.
Values may be sent and summed in bfloat16 or wider, within the bound.
No kernel may reach another device: no remote copies, remote signals or barrier semaphores. Data moves between devices by JAX's collectives and lax.ppermute only.
A program may use at most 128 MiB of HBM per device.

```python
import jax
import jax.numpy as jnp
from jax import lax

D = 768
TILE = 128
BLOCK = 512
CENTERS = 32768
TILE_DEV = 32
DESTS = 16
CAP = 4
BLK_DEV = 8
TILES = 512
ROWS = 65536
N_REGION = 2
N_SHARD = 8


def route_plan(key):
    hotness = jax.random.randint(jax.random.fold_in(key, 11), (DESTS,), 0, 3)
    raw_score = jax.random.randint(jax.random.fold_in(key, 12), (DESTS, DESTS), 0, 4 * DESTS)
    ordered = (raw_score - 2 * DESTS * hotness[None, :]) * DESTS + jnp.arange(DESTS)[None, :]
    ranking = jnp.argsort(ordered, axis=1, stable=True)
    spread = jnp.arange(TILE_DEV) // CAP
    target = ranking[:, spread]
    mixing = jax.random.randint(jax.random.fold_in(key, 13), (DESTS, TILE_DEV), 0, TILE_DEV) * TILE_DEV + jnp.arange(TILE_DEV)[None, :]
    shuffled = jnp.argsort(mixing, axis=1, stable=True)
    target = jnp.take_along_axis(target, shuffled, axis=1)
    inner_id = jax.random.randint(jax.random.fold_in(key, 14), (DESTS, TILE_DEV), 0, BLK_DEV)
    region_id = target // N_SHARD
    block_id = target % N_SHARD * BLK_DEV + inner_id
    return (region_id.reshape(-1).astype(jnp.int32), block_id.reshape(-1).astype(jnp.int32))


def draw_tile_region(key, part):
    region_id, block_id = route_plan(key)
    return region_id


def draw_tile_block(key, part):
    region_id, block_id = route_plan(key)
    return block_id


def with_ends(result, stream_key, low, largest):
    extent = result.shape
    index_at = [jax.random.randint(jax.random.fold_in(stream_key, axis), (), 0, extent[axis]) for axis in range(len(extent))]
    result = result.at[tuple(index_at)].set(low)
    longest = extent.index(max(extent))
    index_at[longest] = (index_at[longest] + 1) % extent[longest]
    return result.at[tuple(index_at)].set(largest)


def levels(own_key, shape, split, least, high):
    loudness, own = 1.0, jax.random.fold_in(own_key, 6)
    for dim, blocks in split:
        steps = jnp.exp(jax.random.uniform(jax.random.fold_in(own, dim), (blocks,), jnp.float32, least / len(split), high / len(split)))
        loudness = loudness * jnp.repeat(steps, shape[dim] // blocks).reshape([-1 if axis == dim else 1 for axis in range(len(shape))])
    return loudness


def scatter_about(rng, extent, scale, reach, pieces=(), kind=jnp.bfloat16):
    values = jax.random.normal(rng, extent, jnp.float32) * scale
    if len(pieces) > 0:
        values = levels(rng, extent, pieces, -0.22, 0.18) * values
    return jnp.clip(values, min=-reach, max=reach).astype(kind)


def setup_inputs(seed: int = 0, part: int = 0) -> dict:
    keys = jax.random.split(jax.random.key(seed), 7)
    part_keys = jax.random.split(jax.random.fold_in(keys[6], part), 7)
    return {
        "vectors": scatter_about(part_keys[0], (ROWS, D), 1.0, 6.0, ((0, 16),)),
        "tile_region": draw_tile_region(jax.random.fold_in(jax.random.fold_in(keys[6], part), 71), part),
        "tile_block": draw_tile_block(jax.random.fold_in(jax.random.fold_in(keys[6], part), 71), part),
        "primary_pick": with_ends(jax.random.randint(part_keys[3], (ROWS,), 0, BLOCK), jax.random.fold_in(part_keys[3], 1), 0, BLOCK - 1).astype(jnp.int32),
        "spill_pick": with_ends(jax.random.randint(part_keys[4], (ROWS,), 0, BLOCK), jax.random.fold_in(part_keys[4], 1), 0, BLOCK - 1).astype(jnp.int32),
        "centers": scatter_about(keys[5], (N_REGION, CENTERS, D), 1.0, 6.0, ((0, 2), (1, 8))),
    }


soar_weight = 1.0
small_term = 1e-5


def score_tile(points, block_rows, primary_idx):
    cross = jnp.dot(points, block_rows.T, preferred_element_type=jnp.float32)
    center_sq = jnp.sum(jnp.square(block_rows.astype(jnp.float32)), axis=1)
    point_f = points.astype(jnp.float32)
    point_sq = jnp.sum(point_f * point_f, axis=1)
    chosen = jnp.take(block_rows, primary_idx, axis=0).astype(jnp.float32)
    residue = point_f - chosen
    residue_sq = jnp.sum(residue * residue, axis=1)
    along = jnp.sum(residue * point_f, axis=1)
    residue_b = residue.astype(jnp.bfloat16)
    against = jnp.dot(residue_b, block_rows.T, preferred_element_type=jnp.float32)
    distance = point_sq[:, None] - 2.0 * cross + center_sq[None, :]
    scale_term = residue_sq / D + small_term
    penalty = jnp.square((along[:, None] - against) / D) / scale_term[:, None]
    spill = (distance / D + soar_weight * penalty).astype(jnp.bfloat16)
    primary = (residue_sq / D).astype(jnp.bfloat16)
    return spill, primary


def reference(vectors, tile_region, tile_block, primary_pick, spill_pick, centers):
    block_count = CENTERS // BLOCK
    all_blocks = centers.reshape(N_REGION * block_count, BLOCK, D)
    block_index = (tile_region * block_count + tile_block).astype(jnp.int32)
    tile_rows = vectors.reshape(TILES, TILE, D)
    primary_rows = primary_pick.reshape(TILES, TILE).astype(jnp.int32)

    def per_tile(packet):
        points, index_one, primary_idx = packet
        block_rows = lax.dynamic_index_in_dim(all_blocks, index_one, 0, keepdims=False)
        return score_tile(points, block_rows, primary_idx)

    spill, primary = lax.map(per_tile, (tile_rows, block_index, primary_rows), batch_size=16)
    spill_scores = spill.reshape(ROWS, BLOCK)
    primary_score = primary.reshape(ROWS)
    spill_chosen = jnp.take_along_axis(spill_scores, spill_pick.astype(jnp.int32)[:, None], axis=1)[:, 0]
    return spill_scores, primary_score, spill_chosen
```

```python
import functools

import jax
import jax.numpy as jnp
from jax import lax
from jax.experimental import pallas as pl
from jax.experimental.pallas import tpu as pltpu
from jax.sharding import PartitionSpec as P

D = 768
TILE = 128
BLOCK = 512
SMALL_TERM = 1e-05
AXES = ("parts", "region", "shard")
F32 = jnp.float32
BF16 = jnp.bfloat16
I32 = jnp.int32
ANY = pl.BlockSpec(memory_space=pl.ANY)
SMEM = pl.BlockSpec(memory_space=pltpu.SMEM)
VMEM = pl.BlockSpec(memory_space=pltpu.VMEM)


def dispatch_kernel(nz, cap, blk_dev, me, region, block, primary, spill, vec, *refs):
    tiles, metas, inv, count, sems = refs[:4], refs[4:8], refs[8], refs[9], refs[10]
    slots = nz * cap
    z, y, core = me[0], me[1], me[2]
    tile_dev = vec.shape[0]
    for d in range(4):
        metas[d][...] = jnp.full(metas[d].shape, -1, I32)

    def clear(i, carry):
        inv[i] = -1
        return carry

    def clear_count(i, carry):
        count[i] = 0
        return carry

    lax.fori_loop(0, 4 * slots, clear, 0)
    lax.fori_loop(0, 4 * nz, clear_count, 0)

    def place(t, carry):
        b = block[t]
        shard = b // blk_dev
        inner = b - shard * blk_dev
        partner = 2 * ((shard & 1) ^ y) + (region[t] ^ core)
        cls = (shard >> 1) ^ z
        at = partner * nz + cls
        rank = count[at]
        count[at] = rank + 1
        slot = cls * cap + rank
        inv[partner * slots + slot] = t
        rows = jnp.concatenate(
            [
                jnp.full((1, TILE), inner, I32),
                primary[pl.ds(t, 1), :],
                spill[pl.ds(t, 1), :],
                jnp.zeros((5, TILE), I32),
            ],
            axis=0,
        )
        for d in range(4):

            @pl.when(partner == d)
            def _():
                metas[d][slot] = rows
                pltpu.make_async_copy(vec.at[t], tiles[d].at[slot], sems.at[t]).start()

        return carry

    lax.fori_loop(0, tile_dev, place, 0)

    def finish(t, carry):
        pltpu.make_async_copy(vec.at[t], tiles[0].at[0], sems.at[t]).wait()
        return carry

    lax.fori_loop(0, tile_dev, finish, 0)


def dispatch(me, region, block, primary, spill, vec, nz, cap, blk_dev):
    slots = nz * cap
    tile_dev = vec.shape[0]
    out = pl.pallas_call(
        functools.partial(dispatch_kernel, nz, cap, blk_dev),
        out_shape=[jax.ShapeDtypeStruct((slots, TILE, D), BF16)] * 4
        + [jax.ShapeDtypeStruct((slots, 8, TILE), I32)] * 4
        + [jax.ShapeDtypeStruct((4 * slots,), I32)],
        in_specs=[SMEM, SMEM, SMEM, VMEM, VMEM, ANY],
        out_specs=[ANY] * 4 + [VMEM] * 4 + [SMEM],
        scratch_shapes=[pltpu.SMEM((4 * nz,), I32), pltpu.SemaphoreType.DMA((tile_dev,))],
        name="dispatch",
    )(me, region, block, primary, spill, vec)
    return out[:4], out[4:8], out[8]


def score_math(points, block_rows, meta):
    picks = meta.astype(F32).T.astype(I32)
    lane = lax.broadcasted_iota(I32, (TILE, BLOCK), 1)
    onehot = (lane == picks[:, 1:2]).astype(F32).astype(BF16)
    chosen = jnp.dot(onehot, block_rows, preferred_element_type=F32)
    point_f = points.astype(F32)
    residue = point_f - chosen
    point_sq = jnp.sum(point_f * point_f, axis=1, keepdims=True)
    residue_sq = jnp.sum(residue * residue, axis=1, keepdims=True)
    along = jnp.sum(residue * point_f, axis=1, keepdims=True)
    both = jnp.concatenate([points, residue.astype(BF16)], axis=0)
    products = lax.dot_general(
        both, block_rows, (((1,), (1,)), ((), ())), preferred_element_type=F32
    )
    cross, against = products[:TILE], products[TILE:]
    block_f = block_rows.astype(F32)
    squares = block_f * block_f
    partial = squares[:, :128]
    for k in range(1, D // 128):
        partial = partial + squares[:, k * 128 : (k + 1) * 128]
    center_sq = jnp.sum(partial.T, axis=0, keepdims=True)
    distance = point_sq - 2.0 * cross + center_sq
    mean_sq = residue_sq / D
    off = (along - against) / D
    scores = (distance / D + off * off * (1.0 / (mean_sq + SMALL_TERM))).astype(BF16)
    picked = jnp.sum(
        jnp.where(lane == picks[:, 2:3], scores.astype(F32), 0.0), axis=1, keepdims=True
    )
    column = lax.broadcasted_iota(I32, (TILE, 128), 1)
    small = jnp.where(column == 0, mean_sq, jnp.where(column == 1, picked, 0.0))
    return scores, small.T[:8]


def score_kernel(nz, cap, blk_dev, sub_blocks, group, order, fetched, me, ids, meta, *refs):
    slots = nz * cap
    wide = len(group) * cap
    n = len(order)
    tiles, refs = refs[:n], refs[n:]
    local, refs = refs[0], refs[1:]
    parts, refs = refs[: len(fetched)], refs[len(fetched) :]
    scores = refs[:n]
    small, work, xbuf, cbuf, obuf, xsem, csem, osem = refs[n:]
    z, half = me[0], me[3]
    half_blocks = blk_dev // 2
    base = group[0] * cap

    total = jnp.int32(0)
    for place, partner in enumerate(order):
        for k in range(wide):
            g = partner * slots + base + k
            work[total] = place * wide + k
            total = total + (ids[g] >= 0).astype(I32)

    def start(i, buf):
        code = work[i]
        place = code // wide
        slot = base + code - place * wide
        partner = jnp.int32(order[0])
        for other in range(1, n):
            partner = jnp.where(place == other, order[other], partner)
        b = ids[partner * slots + slot]
        for other in range(n):

            @pl.when(place == other)
            def _():
                pltpu.make_async_copy(tiles[other].at[slot], xbuf.at[buf], xsem.at[buf]).start()

        step = (z ^ (slot // cap)) - z
        own = b // half_blocks == half
        inside = b % half_blocks
        part = inside // sub_blocks
        row = inside % sub_blocks

        if group[0] == 0:

            @pl.when(step == 0)
            def _():
                pltpu.make_async_copy(local.at[b], cbuf.at[buf], csem.at[buf]).start()

        for ref, (hops, direct, index) in zip(parts, fetched):
            right = own if direct else jnp.logical_not(own)

            @pl.when((step == hops) & right & (part == index))
            def _():
                pltpu.make_async_copy(ref.at[row], cbuf.at[buf], csem.at[buf]).start()

    @pl.when(total > 0)
    def _():
        start(jnp.int32(0), jnp.int32(0))

    def body(i, carry):
        buf = i & 1

        @pl.when(i + 1 < total)
        def _():
            start(i + 1, 1 - buf)

        code = work[i]
        place = code // wide
        k = code - place * wide
        partner = jnp.int32(order[0])
        for other in range(1, n):
            partner = jnp.where(place == other, order[other], partner)
        pltpu.make_async_copy(tiles[0].at[0], xbuf.at[buf], xsem.at[buf]).wait()
        pltpu.make_async_copy(local.at[0], cbuf.at[buf], csem.at[buf]).wait()
        value, rows = score_math(xbuf[buf], cbuf[buf], meta[partner * slots + base + k])
        small[code] = rows

        @pl.when(i >= 2)
        def _():
            pltpu.make_async_copy(obuf.at[buf], scores[0].at[0], osem.at[buf]).wait()

        obuf[buf] = value
        for other in range(n):

            @pl.when(place == other)
            def _():
                pltpu.make_async_copy(obuf.at[buf], scores[other].at[k], osem.at[buf]).start()

        return carry

    lax.fori_loop(0, total, body, 0)

    for back in (2, 1):

        @pl.when(total >= back)
        def _():
            buf = (total - back) & 1
            pltpu.make_async_copy(obuf.at[buf], scores[0].at[0], osem.at[buf]).wait()


def score_call(nz, cap, blk_dev, sub_blocks, group, order, fetched, me, ids, meta, tiles, local, parts):
    wide = len(group) * cap
    n = len(order)
    items = n * wide
    out = pl.pallas_call(
        functools.partial(score_kernel, nz, cap, blk_dev, sub_blocks, group, order, fetched),
        out_shape=[jax.ShapeDtypeStruct((wide, TILE, BLOCK), BF16)] * n
        + [jax.ShapeDtypeStruct((items, 8, TILE), F32)],
        in_specs=[SMEM, SMEM, VMEM] + [ANY] * (n + 1 + len(parts)),
        out_specs=[ANY] * n + [VMEM],
        scratch_shapes=[
            pltpu.SMEM((items + 1,), I32),
            pltpu.VMEM((2, TILE, D), BF16),
            pltpu.VMEM((2, BLOCK, D), BF16),
            pltpu.VMEM((2, TILE, BLOCK), BF16),
            pltpu.SemaphoreType.DMA((2,)),
            pltpu.SemaphoreType.DMA((2,)),
            pltpu.SemaphoreType.DMA((2,)),
        ],
        compiler_params=pltpu.CompilerParams(vmem_limit_bytes=32 * 1024 * 1024),
        cost_estimate=pl.CostEstimate(
            flops=items * 3 * TILE * BLOCK * D, bytes_accessed=items * BLOCK * D, transcendentals=0
        ),
        name="score",
    )(me, ids, meta, *[tiles[p] for p in order], local, *parts)
    return {p: out[i] for i, p in enumerate(order)}, {
        p: out[n][i * wide : (i + 1) * wide] for i, p in enumerate(order)
    }


def assemble_kernel(slots, spans, inv, small, *refs):
    sources, (out, primary, picked, sems) = refs[: len(spans)], refs[len(spans) :]
    for ref, (first, count) in zip(sources, spans):
        for k in range(count):
            g = first + k
            t = inv[g]

            @pl.when(t >= 0)
            def _():
                pltpu.make_async_copy(ref.at[k], out.at[t], sems.at[g]).start()
                rows = small[g]
                primary[pl.ds(t, 1), :] = rows[0:1]
                picked[pl.ds(t, 1), :] = rows[1:2]

    for ref, (first, count) in zip(sources, spans):
        for k in range(count):
            g = first + k
            t = inv[g]

            @pl.when(t >= 0)
            def _():
                pltpu.make_async_copy(ref.at[k], out.at[t], sems.at[g]).wait()


def assemble(tile_dev, slots, spans, inv, small, sources):
    return pl.pallas_call(
        functools.partial(assemble_kernel, slots, spans),
        out_shape=[
            jax.ShapeDtypeStruct((tile_dev, TILE, BLOCK), BF16),
            jax.ShapeDtypeStruct((tile_dev, TILE), F32),
            jax.ShapeDtypeStruct((tile_dev, TILE), F32),
        ],
        in_specs=[SMEM, VMEM] + [ANY] * len(sources),
        out_specs=[ANY, VMEM, VMEM],
        scratch_shapes=[pltpu.SemaphoreType.DMA((4 * slots,))],
        name="assemble",
    )(inv, small, *sources)


def local_part(pieces, vectors, tile_region, tile_block, primary_pick, spill_pick, centers):
    n_parts, n_region, n_shard = (lax.axis_size(a) for a in AXES)
    nz = n_shard // 2
    tile_dev = tile_region.shape[0]
    cap = 2 * tile_dev // (n_region * n_shard)
    slots = nz * cap
    blk_dev = centers.shape[1] // BLOCK
    half_blocks = blk_dev // 2
    pieces = min(pieces, half_blocks)
    sub_blocks = half_blocks // pieces
    shard = lax.axis_index("shard")
    half = lax.axis_index("parts") & 1
    me = jnp.stack([shard >> 1, shard & 1, lax.axis_index("region"), half]).astype(I32)

    def device(p, r, s):
        return (p * n_region + r) * n_shard + s

    every = [(p, r, s) for p in range(n_parts) for r in range(n_region) for s in range(n_shard)]

    def permute(value, target, keep=lambda z: True):
        perm = []
        for p, r, s in every:
            to = target(p, r, s)
            if 0 <= to[2] < n_shard and keep(to[2] >> 1):
                perm.append((device(p, r, s), device(*to)))
        return lax.ppermute(value, AXES, perm)

    local = centers[0].reshape(blk_dev, BLOCK, D)

    own = [
        lax.dynamic_slice_in_dim(local, half * half_blocks + i * sub_blocks, sub_blocks, 0)
        for i in range(pieces)
    ]
    fetched = {}
    moving = {1: own, -1: own}
    for j in range(1, nz):
        for sign in (1, -1):
            keep = (lambda z, j=j: z + j < nz) if sign == 1 else (lambda z, j=j: z >= j)
            moving[sign] = [
                permute(piece, lambda p, r, s: (p, r, s - 2 * sign), keep) for piece in moving[sign]
            ]
            for i, piece in enumerate(moving[sign]):
                fetched[sign * j, True, i] = piece
                fetched[sign * j, False, i] = permute(piece, lambda p, r, s: (p ^ 1, r, s), keep)

    sent, meta_sent, inv = dispatch(
        me,
        tile_region,
        tile_block,
        primary_pick.reshape(tile_dev, TILE),
        spill_pick.reshape(tile_dev, TILE),
        vectors.reshape(tile_dev, TILE, D),
        nz,
        cap,
        blk_dev,
    )

    def exchange(value, partner):
        if partner == 0:
            return value
        return permute(value, lambda p, r, s: (p, r ^ (partner & 1), s ^ (partner >> 1)))

    metas = [exchange(meta_sent[d], d) for d in range(4)]
    tiles = [exchange(sent[d], d) for d in range(4)]
    meta = jnp.concatenate(metas, axis=0)
    ids = meta[:, 0, 0]

    cuts = sorted({0, nz // 2, 3 * nz // 4, nz})
    groups = [tuple(range(a, b)) for a, b in zip(cuts, cuts[1:])]
    spans, sources, smalls = [], [], {d: [] for d in range(4)}
    for group in groups:
        keys = []
        for q in group:
            for z in range(nz):
                hops = (z ^ q) - z
                if hops:
                    for direct in (True, False):
                        keys += [(hops, direct, i) for i in range(pieces)]
        keys = tuple(dict.fromkeys(keys))
        scores, small = score_call(
            nz, cap, blk_dev, sub_blocks, group, (2, 3, 1, 0), keys, me, ids, meta, tiles, local,
            [fetched[k] for k in keys],
        )
        for d in range(4):
            sources.append(exchange(scores[d], d))
            spans.append((d * slots + group[0] * cap, len(group) * cap))
            smalls[d].append(small[d])
    small = jnp.concatenate(
        [exchange(jnp.concatenate(smalls[d], axis=0), d) for d in range(4)], axis=0
    )
    spill_scores, primary, picked = assemble(tile_dev, slots, spans, inv, small, sources)
    return (
        spill_scores.reshape(tile_dev * TILE, BLOCK),
        primary.astype(BF16).reshape(tile_dev * TILE),
        picked.astype(BF16).reshape(tile_dev * TILE),
    )


def solution(mesh):
    rows = P(AXES, None)
    flat = P(AXES)
    return jax.shard_map(
        functools.partial(local_part, 1),
        mesh=mesh,
        in_specs=(rows, flat, flat, flat, flat, P("region", "shard", None)),
        out_specs=(rows, flat, flat),
        check_vma=False,
    )
```

```python
import functools

import jax
import jax.numpy as jnp
from jax import lax
from jax.experimental import pallas as pl
from jax.experimental.pallas import tpu as pltpu
from jax.sharding import PartitionSpec as P

D = 768
TILE = 128
BLOCK = 512
SMALL_TERM = 1e-05
AXES = ("parts", "region", "shard")
F32 = jnp.float32
BF16 = jnp.bfloat16
I32 = jnp.int32
ANY = pl.BlockSpec(memory_space=pl.ANY)
SMEM = pl.BlockSpec(memory_space=pltpu.SMEM)
VMEM_BYTES = 56 * 1024 * 1024
VMEM = pl.BlockSpec(memory_space=pltpu.VMEM)


def ring_place(nz):
    ring = list(range(0, nz, 2))[:1] + list(range(1, nz, 2)) + list(range(2, nz, 2))[::-1]
    return ring, [ring.index(z) for z in range(nz)]


def place_of(z, nz):
    return jnp.where(z == 0, 0, jnp.where(z & 1 == 1, (z + 1) // 2, nz - z // 2))


def plan_kernel(nz, cap, blk_dev, me, region, block, primary, spill, *refs):
    metas, at_slot, inv, count = refs[:4], refs[4], refs[5], refs[6]
    slots = nz * cap
    at_ring, y, core = me[0], me[1], me[2]
    for d in range(4):
        metas[d][...] = jnp.full(metas[d].shape, -1, I32)

    def clear(i, carry):
        inv[i] = -1
        return carry

    def clear_count(i, carry):
        count[i] = 0
        return carry

    lax.fori_loop(0, 4 * slots, clear, 0)
    lax.fori_loop(0, 4 * nz, clear_count, 0)

    def place(t, carry):
        b = block[t]
        shard = b // blk_dev
        inner = b - shard * blk_dev
        partner = 2 * ((shard & 1) ^ y) + (region[t] ^ core)
        cls = lax.rem(at_ring - place_of(shard >> 1, nz) + nz, nz)
        at = partner * nz + cls
        rank = count[at]
        count[at] = rank + 1
        slot = cls * cap + rank
        inv[partner * slots + slot] = t
        at_slot[t] = partner * slots + slot
        rows = jnp.concatenate(
            [
                jnp.full((1, TILE), inner, I32),
                primary[pl.ds(t, 1), :],
                spill[pl.ds(t, 1), :],
                jnp.zeros((5, TILE), I32),
            ],
            axis=0,
        )
        for d in range(4):

            @pl.when(partner == d)
            def _():
                metas[d][slot] = rows

        return carry

    lax.fori_loop(0, region.shape[0], place, 0)


def plan(me, region, block, primary, spill, nz, cap, blk_dev):
    slots = nz * cap
    out = pl.pallas_call(
        functools.partial(plan_kernel, nz, cap, blk_dev),
        out_shape=[jax.ShapeDtypeStruct((slots, 8, TILE), I32)] * 4
        + [
            jax.ShapeDtypeStruct(region.shape, I32),
            jax.ShapeDtypeStruct((4 * slots,), I32),
        ],
        in_specs=[SMEM, SMEM, SMEM, VMEM, VMEM],
        out_specs=[VMEM] * 4 + [SMEM, SMEM],
        scratch_shapes=[pltpu.SMEM((4 * nz,), I32)],
        name="plan",
    )(me, region, block, primary, spill)
    return out[:4], out[4], out[5]


def dispatch_kernel(slots, at_slot, vec, *refs):
    refs = refs[4:]
    tiles, (held, in_sems, out_sems) = refs[:5], refs[5:]
    tile_dev = vec.shape[0]
    part = slots // 2

    def each(act):
        def body(t, carry):
            partner = at_slot[t] // slots

            @pl.when(partner > 0)
            def _():
                act(t, at_slot[t])

            return carry

        lax.fori_loop(0, tile_dev, body, 0)

    def bring(t, g):
        pltpu.make_async_copy(vec.at[t], held.at[t], in_sems.at[t]).start()

    def send(t, g):
        pltpu.make_async_copy(vec.at[t], held.at[t], in_sems.at[t]).wait()
        for i, first in enumerate((slots, 2 * slots, 2 * slots + part, 3 * slots, 3 * slots + part)):
            count = slots if i == 0 else part

            @pl.when((g >= first) & (g < first + count))
            def _():
                pltpu.make_async_copy(held.at[t], tiles[i].at[g - first], out_sems.at[t]).start()

    def finish(t, g):
        pltpu.make_async_copy(held.at[t], tiles[0].at[0], out_sems.at[t]).wait()

    each(bring)
    each(send)
    each(finish)


def dispatch(at_slot, vec, metas, slots):
    tile_dev = vec.shape[0]
    return pl.pallas_call(
        functools.partial(dispatch_kernel, slots),
        out_shape=[
            jax.ShapeDtypeStruct((n, TILE, D), BF16) for n in (slots,) + (slots // 2,) * 4
        ],
        in_specs=[SMEM, ANY] + [ANY] * 4,
        out_specs=[ANY] * 5,
        scratch_shapes=[
            pltpu.VMEM((tile_dev, TILE, D), BF16),
            pltpu.SemaphoreType.DMA((tile_dev,)),
            pltpu.SemaphoreType.DMA((tile_dev,)),
        ],
        compiler_params=pltpu.CompilerParams(vmem_limit_bytes=VMEM_BYTES),
        name="dispatch",
    )(at_slot, vec, *metas)


def gate_kernel(*refs):
    pass


def gate(passed, others):
    n = len(passed)
    return pl.pallas_call(
        gate_kernel,
        out_shape=[jax.ShapeDtypeStruct(v.shape, v.dtype) for v in passed],
        in_specs=[ANY] * (n + len(others)),
        out_specs=[ANY] * n,
        input_output_aliases={i: i for i in range(n)},
        compiler_params=pltpu.CompilerParams(vmem_limit_bytes=VMEM_BYTES),
        name="gate",
    )(*passed, *others)


def score_math(points, block_rows, meta):
    picks = meta.astype(F32).T.astype(I32)
    lane = lax.broadcasted_iota(I32, (TILE, BLOCK), 1)
    onehot = (lane == picks[:, 1:2]).astype(F32).astype(BF16)
    chosen = jnp.dot(onehot, block_rows, preferred_element_type=F32)
    point_f = points.astype(F32)
    residue = point_f - chosen
    point_sq = jnp.sum(point_f * point_f, axis=1, keepdims=True)
    residue_sq = jnp.sum(residue * residue, axis=1, keepdims=True)
    along = jnp.sum(residue * point_f, axis=1, keepdims=True)
    both = jnp.concatenate([points, residue.astype(BF16)], axis=0)
    products = lax.dot_general(
        both, block_rows, (((1,), (1,)), ((), ())), preferred_element_type=F32
    )
    cross, against = products[:TILE], products[TILE:]
    block_f = block_rows.astype(F32)
    squares = block_f * block_f
    partial = squares[:, :128]
    for k in range(1, D // 128):
        partial = partial + squares[:, k * 128 : (k + 1) * 128]
    center_sq = jnp.sum(partial.T, axis=0, keepdims=True)
    distance = point_sq - 2.0 * cross + center_sq
    mean_sq = residue_sq / D
    off = (along - against) / D
    scores = (distance / D + off * off * (1.0 / (mean_sq + SMALL_TERM))).astype(BF16)
    picked = jnp.sum(
        jnp.where(lane == picks[:, 2:3], scores.astype(F32), 0.0), axis=1, keepdims=True
    )
    column = lax.broadcasted_iota(I32, (TILE, 128), 1)
    small = jnp.where(column == 0, mean_sq, jnp.where(column == 1, picked, 0.0))
    return scores, small.T[:8]


def score_kernel(nz, cap, blk_dev, sub_blocks, group, order, fetched, bases, me, ids, inv, meta, *refs):
    slots = nz * cap
    wide = len(group) * cap
    n = len(order)
    tiles, refs = refs[:n], refs[n:]
    local, refs = refs[0], refs[1:]
    before, refs = (refs[:n], refs[n:]) if group[0] else ((), refs)
    parts, refs = refs[: len(fetched)], refs[len(fetched) :]
    scores, smalls = refs[:n], refs[n : 2 * n]
    work, xbuf, cbuf, obuf, xsem, csem, osem = refs[2 * n :]
    half = me[3]
    half_blocks = blk_dev // 2
    base = group[0] * cap
    for old, new in zip(before, smalls):
        new[...] = old[...]

    total = jnp.int32(0)
    for place, partner in enumerate(order):
        for k in range(wide):
            g = partner * slots + base + k
            work[total] = place * wide + k
            total = total + (ids[g] >= 0).astype(I32)

    def start(i, buf):
        code = work[i]
        place = code // wide
        slot = base + code - place * wide
        partner = jnp.int32(order[0])
        for other in range(1, n):
            partner = jnp.where(place == other, order[other], partner)
        b = ids[partner * slots + slot]
        for other in range(n):
            row = slot - bases[other] if order[other] else jnp.maximum(inv[slot], 0)

            @pl.when(place == other)
            def _():
                pltpu.make_async_copy(tiles[other].at[row], xbuf.at[buf], xsem.at[buf]).start()

        cls = slot // cap
        own = b // half_blocks == half
        inside = b % half_blocks
        part = inside // sub_blocks
        row = inside % sub_blocks

        if group[0] == 0:

            @pl.when(cls == 0)
            def _():
                pltpu.make_async_copy(local.at[b], cbuf.at[buf], csem.at[buf]).start()

        for ref, (hops, direct, index) in zip(parts, fetched):
            right = own if direct else jnp.logical_not(own)

            @pl.when((cls == hops) & right & (part == index))
            def _():
                pltpu.make_async_copy(ref.at[row], cbuf.at[buf], csem.at[buf]).start()

    @pl.when(total > 0)
    def _():
        start(jnp.int32(0), jnp.int32(0))

    def body(i, carry):
        buf = i & 1

        @pl.when(i + 1 < total)
        def _():
            start(i + 1, 1 - buf)

        code = work[i]
        place = code // wide
        k = code - place * wide
        partner = jnp.int32(order[0])
        for other in range(1, n):
            partner = jnp.where(place == other, order[other], partner)
        pltpu.make_async_copy(tiles[0].at[0], xbuf.at[buf], xsem.at[buf]).wait()
        pltpu.make_async_copy(local.at[0], cbuf.at[buf], csem.at[buf]).wait()
        value, rows = score_math(xbuf[buf], cbuf[buf], meta[partner * slots + base + k])
        @pl.when(i >= 2)
        def _():
            pltpu.make_async_copy(obuf.at[buf], scores[0].at[0], osem.at[buf]).wait()

        obuf[buf] = value
        for other in range(n):

            @pl.when(place == other)
            def _():
                smalls[other][base + k] = rows
                pltpu.make_async_copy(obuf.at[buf], scores[other].at[k], osem.at[buf]).start()

        return carry

    lax.fori_loop(0, total, body, 0)

    for back in (2, 1):

        @pl.when(total >= back)
        def _():
            buf = (total - back) & 1
            pltpu.make_async_copy(obuf.at[buf], scores[0].at[0], osem.at[buf]).wait()


def score_call(
    nz, cap, blk_dev, sub_blocks, group, order, fetched, bases, me, ids, inv, meta, tiles, local, before, parts
):
    wide = len(group) * cap
    n = len(order)
    items = n * wide
    out = pl.pallas_call(
        functools.partial(score_kernel, nz, cap, blk_dev, sub_blocks, group, order, fetched, bases),
        out_shape=[jax.ShapeDtypeStruct((wide, TILE, BLOCK), BF16)] * n
        + [jax.ShapeDtypeStruct((nz * cap, 8, TILE), F32)] * n,
        in_specs=[SMEM, SMEM, SMEM, VMEM]
        + [ANY] * (n + 1)
        + [VMEM] * len(before)
        + [ANY] * len(parts),
        out_specs=[ANY] * n + [VMEM] * n,
        scratch_shapes=[
            pltpu.SMEM((items + 1,), I32),
            pltpu.VMEM((2, TILE, D), BF16),
            pltpu.VMEM((2, BLOCK, D), BF16),
            pltpu.VMEM((2, TILE, BLOCK), BF16),
            pltpu.SemaphoreType.DMA((2,)),
            pltpu.SemaphoreType.DMA((2,)),
            pltpu.SemaphoreType.DMA((2,)),
        ],
        compiler_params=pltpu.CompilerParams(vmem_limit_bytes=VMEM_BYTES),
        cost_estimate=pl.CostEstimate(
            flops=items * 3 * TILE * BLOCK * D, bytes_accessed=items * BLOCK * D, transcendentals=0
        ),
        name="score",
    )(me, ids, inv, meta, *tiles, local, *before, *parts)
    return out[:n], out[n:]


def assemble_kernel(first, wide, n_before, slots, inv, *refs):
    n = len(first)
    sources, refs = refs[:n], refs[n + n_before :]
    smalls, refs = (refs[:4], refs[4:]) if slots else ((), refs)
    out, refs = refs[0], refs[1:]
    (primary, picked), refs = (refs[:2], refs[2:]) if slots else ((None, None), refs)
    held, in_sems, out_sems = refs

    def each(act):
        for d in range(n):
            for k in range(wide):
                t = inv[first[d] + k]

                @pl.when(t >= 0)
                def _():
                    act(d, k, t, d * wide + k)

    def bring(d, k, t, n):
        pltpu.make_async_copy(sources[d].at[k], held.at[n], in_sems.at[n]).start()

    def send(d, k, t, n):
        pltpu.make_async_copy(sources[d].at[k], held.at[n], in_sems.at[n]).wait()
        pltpu.make_async_copy(held.at[n], out.at[t], out_sems.at[n]).start()

    def finish(d, k, t, n):
        pltpu.make_async_copy(held.at[n], out.at[t], out_sems.at[n]).wait()

    each(bring)
    for d, small in enumerate(smalls):
        for k in range(slots):
            t = inv[d * slots + k]

            @pl.when(t >= 0)
            def _():
                primary[pl.ds(t, 1), :] = small[k, 0:1, :]
                picked[pl.ds(t, 1), :] = small[k, 1:2, :]

    each(send)
    each(finish)


def assemble(tile_dev, first, wide, inv, sources, before, smalls=()):
    count = len(first) * wide
    n = len(sources)
    slots = smalls[0].shape[0] if smalls else 0
    rows = [jax.ShapeDtypeStruct((tile_dev, TILE), F32)] * 2 if smalls else []
    return pl.pallas_call(
        functools.partial(assemble_kernel, first, wide, len(before), slots),
        out_shape=[jax.ShapeDtypeStruct((tile_dev, TILE, BLOCK), BF16)] + rows,
        in_specs=[SMEM] + [ANY] * (n + len(before)) + [VMEM] * len(smalls),
        out_specs=[ANY] + [VMEM] * len(rows),
        scratch_shapes=[
            pltpu.VMEM((count, TILE, BLOCK), BF16),
            pltpu.SemaphoreType.DMA((count,)),
            pltpu.SemaphoreType.DMA((count,)),
        ],
        input_output_aliases={1 + n: 0} if before else {},
        compiler_params=pltpu.CompilerParams(vmem_limit_bytes=VMEM_BYTES),
        name="assemble",
    )(inv, *sources, *before, *smalls)


def local_part(pieces, vectors, tile_region, tile_block, primary_pick, spill_pick, centers):
    n_parts, n_region, n_shard = (lax.axis_size(a) for a in AXES)
    nz = n_shard // 2
    tile_dev = tile_region.shape[0]
    cap = 2 * tile_dev // (n_region * n_shard)
    slots = nz * cap
    blk_dev = centers.shape[1] // BLOCK
    half_blocks = blk_dev // 2
    pieces = min(pieces, half_blocks)
    sub_blocks = half_blocks // pieces
    shard = lax.axis_index("shard")
    half = lax.axis_index("parts") & 1
    ring, at_ring = ring_place(nz)
    me = jnp.stack(
        [place_of(shard >> 1, nz), shard & 1, lax.axis_index("region"), half]
    ).astype(I32)

    def device(p, r, s):
        return (p * n_region + r) * n_shard + s

    every = [(p, r, s) for p in range(n_parts) for r in range(n_region) for s in range(n_shard)]

    def permute(value, target):
        return lax.ppermute(value, AXES, [(device(*a), device(*target(*a))) for a in every])

    def next_z(p, r, s):
        return (p, r, 2 * ring[(at_ring[s >> 1] + 1) % nz] + (s & 1))

    def other_part(p, r, s):
        return (p ^ 1, r, s)

    local = centers[0].reshape(blk_dev, BLOCK, D)

    tile_rows = vectors.reshape(tile_dev, TILE, D)
    meta_sent, at_slot, inv = plan(
        me,
        tile_region,
        tile_block,
        primary_pick.reshape(tile_dev, TILE),
        spill_pick.reshape(tile_dev, TILE),
        nz,
        cap,
        blk_dev,
    )

    def exchange(value, partner):
        if partner == 0:
            return value
        return permute(value, lambda p, r, s: (p, r ^ (partner & 1), s ^ (partner >> 1)))

    metas = [exchange(meta_sent[d], d) for d in range(4)]
    meta = jnp.concatenate(metas, axis=0)
    ids = meta[:, 0, 0]
    sent = dispatch(at_slot, tile_rows, metas, slots)

    env, waits, opens = {}, {}, {}

    def send(name, payload, target, done):
        env[name] = permute(env[payload], target)
        waits.setdefault(done, []).append(name)

    def hold(name, value, until):
        env[name] = value
        opens.setdefault(until, []).append(name)

    def across(d):
        return lambda p, r, s: (p, r ^ (d & 1), s ^ (d >> 1))

    steps = (nz - 1) * pieces
    last = steps + 1
    tile_gates = [min(steps, (j * pieces + 1) // 2 + 1) for j in range(1, 5)]
    tile_names = [("t", 2, 0), ("t", 3, 0), ("t", 2, 1), ("t", 3, 1)]
    for j, name in enumerate(tile_names):
        value = sent[1 + 2 * (name[1] - 2) + name[2]]
        hold(("sent",) + name[1:], value, 0 if j < 2 else tile_gates[j - 2])
    for i in range(pieces):
        hold(
            ("own", i),
            lax.dynamic_slice_in_dim(local, half * half_blocks + i * sub_blocks, sub_blocks, 0),
            0,
        )
    env["core"] = sent[0]
    send(("t", 1, 0), "core", across(1), tile_gates[0])
    cuts = sorted({0, nz // 2, 3 * nz // 4, nz})
    groups = [tuple(range(a, b)) for a, b in zip(cuts, cuts[1:])]
    ready = [max(tile_gates[1], (groups[0][-1]) * pieces + 1)]
    ready += [max(tile_gates[3], group[-1] * pieces + 1) for group in groups[1:]]
    smalls = {}
    output = ()

    def score(n, order):
        group = groups[n]
        part = 1 if 2 * group[0] >= nz else 0
        keys = tuple(
            (hops, direct, i)
            for hops in group
            if hops > 0
            for direct in (True, False)
            for i in range(pieces)
        )
        tiles = [tile_rows if d == 0 else env["t", d, part if d > 1 else 0] for d in order]
        bases = [part * slots // 2 if d > 1 else 0 for d in order]
        scores, small = score_call(
            nz, cap, blk_dev, sub_blocks, group, order, keys, bases, me, ids, inv, meta, tiles, local,
            [smalls[d] for d in order] if n else [],
            [env[("z" if direct else "x"), (hops - 1) * pieces + i + 1] for hops, direct, i in keys],
        )
        for d, values, rows in zip(order, scores, small):
            env["s", n, d] = values
            smalls[d] = rows

    def place(n, before, with_smalls=()):
        wide = len(groups[n]) * cap
        return assemble(
            tile_dev,
            [d * slots + groups[n][0] * cap for d in range(4)],
            wide,
            inv,
            [env["s", n, 0]] + [env["r", n, d] for d in (1, 2, 3)],
            before,
            with_smalls,
        )

    stride = max(1, pieces // 2)
    back = {
        (0, 2): (tile_gates[2], tile_gates[3] + stride),
        (0, 3): (tile_gates[3], last),
        (0, 1): (tile_gates[3], tile_gates[3] + stride),
        (1, 2): (tile_gates[3] + stride, last),
        (1, 3): (tile_gates[3] + stride, last),
        (1, 1): (tile_gates[3] + stride, last),
    }
    for key, (begin, end) in back.items():
        begin = max(begin, ready[key[0]] + 1)
        back[key] = begin, max(end, begin + 1)
    scored = 0
    for k in range(last + 1):
        if k:
            passed = waits.get(k, []) + opens.get(k, [])
            passed = [name for name in passed if name in env]
            for name, value in zip(passed, gate([env[n] for n in passed], [])):
                env[name] = value
        if k == 0:
            for i in range(min(pieces, steps)):
                send(("z", i + 1), ("own", i), next_z, i + 1)
            for name in tile_names[:2]:
                send(name, ("sent",) + name[1:], across(name[1]), tile_gates[tile_names.index(name)])
        elif k <= steps:
            if k + pieces <= steps:
                send(("z", k + pieces), ("z", k), next_z, k + pieces)
            send(("x", k), ("z", k), other_part, k + 1)
        for j in (2, 3):
            if k and k == tile_gates[j - 2]:
                send(tile_names[j], ("sent",) + tile_names[j][1:], across(tile_names[j][1]), tile_gates[j])
        for (n, d), (begin, end) in back.items():
            if k and begin == k and n < scored:
                send(("r", n, d), ("s", n, d), across(d), end)
        while scored < len(groups) and k == ready[scored]:
            score(scored, (2, 3))
            if scored < len(groups) - 1:
                score(scored, (1, 0))
                for d in (1, 2, 3):
                    opens.setdefault(back[scored, d][0], []).append(("s", scored, d))
            scored += 1
    n = len(groups) - 1
    for d in (2, 3):
        env["r", n, d] = exchange(env["s", n, d], d)
        smalls[d] = exchange(smalls[d], d)
    score(n, (1, 0))
    env["r", n, 1] = exchange(env["s", n, 1], 1)
    smalls[1] = exchange(smalls[1], 1)
    before = []
    for i in range(n):
        before = [place(i, before)[0]]
    spill_scores, primary, picked = place(n, before, [smalls[d] for d in range(4)])
    return (
        spill_scores.reshape(tile_dev * TILE, BLOCK),
        primary.astype(BF16).reshape(tile_dev * TILE),
        picked.astype(BF16).reshape(tile_dev * TILE),
    )


def solution(mesh):
    rows = P(AXES, None)
    flat = P(AXES)
    return jax.shard_map(
        functools.partial(local_part, 2),
        mesh=mesh,
        in_specs=(rows, flat, flat, flat, flat, P("region", "shard", None)),
        out_specs=(rows, flat, flat),
        check_vma=False,
    )
```

```python
import functools

import jax
import jax.numpy as jnp
from jax import lax
from jax.experimental import pallas as pl
from jax.experimental.pallas import tpu as pltpu
from jax.sharding import PartitionSpec as P

D = 768
TILE = 128
BLOCK = 512
SMALL_TERM = 1e-05
AXES = ("parts", "region", "shard")
F32 = jnp.float32
BF16 = jnp.bfloat16
I32 = jnp.int32
ANY = pl.BlockSpec(memory_space=pl.ANY)
SMEM = pl.BlockSpec(memory_space=pltpu.SMEM)
SHORT = pl.CostEstimate(flops=1, bytes_accessed=1, transcendentals=0)
VMEM_BYTES = 62 * 1024 * 1024
VMEM = pl.BlockSpec(memory_space=pltpu.VMEM)


def ring_place(nz):
    ring = list(range(0, nz, 2))[:1] + list(range(1, nz, 2)) + list(range(2, nz, 2))[::-1]
    return ring, [ring.index(z) for z in range(nz)]


def place_of(z, nz):
    return jnp.where(z == 0, 0, jnp.where(z & 1 == 1, (z + 1) // 2, nz - z // 2))


def slot_of(nz, cap, blk_dev, at_ring, y, core, region, block):
    shard = block // blk_dev
    partner = 2 * ((shard & 1) ^ y) + (region ^ core)
    cls = lax.rem(at_ring - place_of(shard >> 1, nz) + nz, nz)
    at = partner * nz + cls
    return partner, cls * cap, at


def zero(ref, n):
    def body(i, carry):
        ref[i] = 0
        return carry

    lax.fori_loop(0, n, body, 0)


def plan_kernel(nz, cap, blk_dev, n_before, me, region, block, *refs):
    at_slot, inv, count = refs[n_before:]
    slots = nz * cap

    def clear(i, carry):
        inv[i] = -1
        return carry

    lax.fori_loop(0, 4 * slots, clear, 0)
    zero(count, 4 * nz)

    def place(t, carry):
        partner, first, at = slot_of(nz, cap, blk_dev, me[0], me[1], me[2], region[t], block[t])
        rank = count[at]
        count[at] = rank + 1
        g = partner * slots + first + rank
        inv[g] = t
        at_slot[t] = g
        return carry

    lax.fori_loop(0, region.shape[0], place, 0)


def plan(me, region, block, before, nz, cap, blk_dev):
    return pl.pallas_call(
        functools.partial(plan_kernel, nz, cap, blk_dev, len(before)),
        out_shape=[
            jax.ShapeDtypeStruct(region.shape, I32),
            jax.ShapeDtypeStruct((4 * nz * cap,), I32),
        ],
        in_specs=[SMEM, SMEM, SMEM] + [ANY] * len(before),
        out_specs=[SMEM, SMEM],
        scratch_shapes=[pltpu.SMEM((4 * nz,), I32)],
        compiler_params=pltpu.CompilerParams(vmem_limit_bytes=VMEM_BYTES),
        cost_estimate=SHORT,
        name="plan",
    )(me, region, block, *before)


def receive_kernel(nz, cap, blk_dev, tile_dev, me, *refs):
    packs, (meta, ids, held, scalars, count, held_sems, scalar_sems) = refs[:4], refs[4:]
    slots = nz * cap
    at_ring, y, core = me[0], me[1], me[2]

    def copies(d):
        return (
            pltpu.make_async_copy(packs[d], held.at[d], held_sems.at[d]),
            pltpu.make_async_copy(packs[d].at[pl.ds(2 * tile_dev, 8)], scalars.at[d], scalar_sems.at[d]),
        )

    for d in range(4):
        for copy in copies(d):
            copy.start()

    def clear(i, carry):
        ids[i] = -1
        return carry

    lax.fori_loop(0, 4 * slots, clear, 0)
    for d in range(4):
        for copy in copies(d):
            copy.wait()
        zero(count, 4 * nz)

        def place(t, carry):
            block = scalars[d, 1, t]
            partner, first, at = slot_of(
                nz, cap, blk_dev, at_ring, y ^ (d >> 1), core ^ (d & 1), scalars[d, 0, t], block
            )

            @pl.when(partner == d)
            def _():
                rank = count[at]
                count[at] = rank + 1
                g = d * slots + first + rank
                ids[g] = lax.rem(block, blk_dev)
                meta[g, 1:2, :] = held[d, pl.ds(t, 1), :]
                meta[g, 2:3, :] = held[d, pl.ds(tile_dev + t, 1), :]

            return carry

        lax.fori_loop(0, tile_dev, place, 0)


def receive(me, packs, nz, cap, blk_dev, tile_dev):
    slots = nz * cap
    return pl.pallas_call(
        functools.partial(receive_kernel, nz, cap, blk_dev, tile_dev),
        out_shape=[
            jax.ShapeDtypeStruct((4 * slots, 8, TILE), I32),
            jax.ShapeDtypeStruct((4 * slots,), I32),
        ],
        in_specs=[SMEM] + [ANY] * 4,
        out_specs=[VMEM, SMEM],
        scratch_shapes=[
            pltpu.VMEM((4,) + packs[0].shape, I32),
            pltpu.SMEM((4, 8, TILE), I32),
            pltpu.SMEM((4 * nz,), I32),
            pltpu.SemaphoreType.DMA((4,)),
            pltpu.SemaphoreType.DMA((4,)),
        ],
        compiler_params=pltpu.CompilerParams(vmem_limit_bytes=VMEM_BYTES),
        cost_estimate=SHORT,
        name="receive",
    )(me, *packs)


def dispatch_kernel(slots, runs, n_before, at_slot, vec, *refs):
    refs = refs[n_before:]
    tiles, (held, in_sems, out_sems) = refs[: len(runs)], refs[len(runs) :]
    tile_dev = vec.shape[0]

    def each(act):
        def body(t, carry):
            g = at_slot[t]

            @pl.when(g >= slots)
            def _():
                act(t, g)

            return carry

        lax.fori_loop(0, tile_dev, body, 0)

    def bring(t, g):
        pltpu.make_async_copy(vec.at[t], held.at[t], in_sems.at[t]).start()

    def send(t, g):
        pltpu.make_async_copy(vec.at[t], held.at[t], in_sems.at[t]).wait()
        for ref, (d, first, count) in zip(tiles, runs):
            begin = d * slots + first

            @pl.when((g >= begin) & (g < begin + count))
            def _():
                pltpu.make_async_copy(held.at[t], ref.at[g - begin], out_sems.at[t]).start()

    def finish(t, g):
        pltpu.make_async_copy(held.at[t], tiles[0].at[0], out_sems.at[t]).wait()

    each(bring)
    each(send)
    each(finish)


def dispatch(at_slot, vec, before, slots, runs):
    tile_dev = vec.shape[0]
    return pl.pallas_call(
        functools.partial(dispatch_kernel, slots, runs, len(before)),
        out_shape=[jax.ShapeDtypeStruct((count, TILE, D), BF16) for _, _, count in runs],
        in_specs=[SMEM, ANY] + [ANY] * len(before),
        out_specs=[ANY] * len(runs),
        scratch_shapes=[
            pltpu.VMEM((tile_dev, TILE, D), BF16),
            pltpu.SemaphoreType.DMA((tile_dev,)),
            pltpu.SemaphoreType.DMA((tile_dev,)),
        ],
        compiler_params=pltpu.CompilerParams(vmem_limit_bytes=VMEM_BYTES),
        cost_estimate=SHORT,
        name="dispatch",
    )(at_slot, vec, *before)


def gate_kernel(*refs):
    pass


def gate(passed):
    n = len(passed)
    return pl.pallas_call(
        gate_kernel,
        out_shape=[jax.ShapeDtypeStruct(v.shape, v.dtype) for v in passed],
        in_specs=[ANY] * n,
        out_specs=[ANY] * n,
        input_output_aliases={i: i for i in range(n)},
        compiler_params=pltpu.CompilerParams(vmem_limit_bytes=VMEM_BYTES),
        cost_estimate=SHORT,
        name="gate",
    )(*passed)


def score_math(points, block_rows, meta):
    picks = meta.astype(F32).T.astype(I32)
    lane = lax.broadcasted_iota(I32, (TILE, BLOCK), 1)
    onehot = (lane == picks[:, 1:2]).astype(F32).astype(BF16)
    chosen = jnp.dot(onehot, block_rows, preferred_element_type=F32)
    point_f = points.astype(F32)
    residue = point_f - chosen
    point_sq = jnp.sum(point_f * point_f, axis=1, keepdims=True)
    residue_sq = jnp.sum(residue * residue, axis=1, keepdims=True)
    along = jnp.sum(residue * point_f, axis=1, keepdims=True)
    both = jnp.concatenate([points, residue.astype(BF16)], axis=0)
    products = lax.dot_general(
        both, block_rows, (((1,), (1,)), ((), ())), preferred_element_type=F32
    )
    cross, against = products[:TILE], products[TILE:]
    block_f = block_rows.astype(F32)
    squares = block_f * block_f
    partial = squares[:, :128]
    for k in range(1, D // 128):
        partial = partial + squares[:, k * 128 : (k + 1) * 128]
    center_sq = jnp.sum(partial.T, axis=0, keepdims=True)
    distance = point_sq - 2.0 * cross + center_sq
    mean_sq = residue_sq / D
    off = (along - against) / D
    scores = (distance / D + off * off * (1.0 / (mean_sq + SMALL_TERM))).astype(BF16)
    picked = jnp.sum(
        jnp.where(lane == picks[:, 2:3], scores.astype(F32), 0.0), axis=1, keepdims=True
    )
    column = lax.broadcasted_iota(I32, (TILE, 128), 1)
    small = jnp.where(column == 0, mean_sq, jnp.where(column == 1, picked, 0.0))
    return scores, small.T[:8]


def score_kernel(nz, cap, blk_dev, group, order, runs, fetched, late, resident, aliased, n_extra, me, ids, inv, meta, *refs):
    slots = nz * cap
    wide = len(group) * cap
    n = len(order)
    tiles, refs = refs[: len(runs)], refs[len(runs) :]
    local, parts = refs[0], refs[1 : 1 + len(fetched)]
    refs = refs[1 + len(fetched) + aliased + n_extra :]
    scores = refs[:n]
    work, xbuf, cbuf, obuf, tail, tail_b, xsem, csem, osem, tsem = refs[n:]
    half = me[3]
    half_blocks = blk_dev // 2
    base = group[0] * cap

    total = jnp.int32(0)
    for place, partner in enumerate(order):
        for k in range(wide):
            b = ids[partner * slots + base + k]
            valid = b >= 0
            if late is not None:
                first, wanted = late
                is_late = (b // half_blocks != half) & (b % half_blocks >= first)
                is_late = is_late & (group[k // cap] == nz - 1)
                valid = valid & (is_late == wanted)
            work[total] = place * wide + k
            total = total + valid.astype(I32)

    def start(i):
        code = work[i]
        place = code // wide
        slot = base + code - place * wide
        partner = jnp.int32(order[0])
        for other in range(1, n):
            partner = jnp.where(place == other, order[other], partner)
        b = ids[partner * slots + slot]
        for ref, (d, first, count) in zip(tiles, runs):
            row = slot - first if d else jnp.maximum(inv[slot], 0)

            @pl.when((partner == d) & (slot >= first) & (slot < first + count))
            def _():
                pltpu.make_async_copy(ref.at[row], xbuf.at[i], xsem.at[i]).start()

        cls = slot // cap
        own = b // half_blocks == half
        inside = b % half_blocks

        if resident:
            return

        if group[0] == 0:

            @pl.when(cls == 0)
            def _():
                pltpu.make_async_copy(local.at[b], cbuf.at[i], csem.at[i]).start()

        for ref, (hops, direct, first, count) in zip(parts, fetched):
            right = own if direct else jnp.logical_not(own)

            @pl.when((cls == hops) & right & (inside >= first) & (inside < first + count))
            def _():
                pltpu.make_async_copy(ref.at[inside - first], cbuf.at[i], csem.at[i]).start()

    def begin(i, carry):
        start(i)
        return carry

    lax.fori_loop(0, total, begin, 0)
    tail_rows = pl.ds(wide * TILE + 16 * (aliased > 0), 16)
    tail[...] = jnp.zeros(tail.shape, F32)

    def centers_of(i, slot, partner):
        if not resident:
            return cbuf[i]
        inside = ids[partner * slots + slot] % half_blocks
        rows = parts[0][jnp.clip(inside - fetched[0][2], 0, fetched[0][3] - 1)]
        for ref, (hops, direct, first, count) in zip(parts[1:], fetched[1:]):
            rows = jnp.where(inside >= first, ref[jnp.clip(inside - first, 0, count - 1)], rows)
        return rows

    def where(i):
        code = work[i]
        place = code // wide
        partner = jnp.int32(order[0])
        for other in range(1, n):
            partner = jnp.where(place == other, order[other], partner)
        return place, code - place * wide, partner

    def body(pair, carry):
        both = (2 * pair, jnp.minimum(2 * pair + 1, total - 1))
        spots = [where(i) for i in both]
        values = []
        for j, i in enumerate(both):

            @pl.when(2 * pair + j < total)
            def _():
                pltpu.make_async_copy(tiles[0].at[0], xbuf.at[i], xsem.at[i]).wait()
                if not resident:
                    pltpu.make_async_copy(local.at[0], cbuf.at[i], csem.at[i]).wait()

        for i, (place, k, partner) in zip(both, spots):
            rows = centers_of(i, base + k, partner)
            values.append(score_math(xbuf[i], rows, meta[partner * slots + base + k]))
        for i, (place, k, partner), (value, rows) in zip(both, spots, values):
            obuf[i] = value
            tail[place, pl.ds(k, 1), 0 : 2 * TILE] = jnp.concatenate([rows[0:1], rows[1:2]], axis=1)
        for j, (i, (place, k, partner)) in enumerate(zip(both, spots)):
            for other in range(n):

                @pl.when((place == other) & (2 * pair + j < total))
                def _():
                    pltpu.make_async_copy(
                        obuf.at[i], scores[other].at[pl.ds(k * TILE, TILE)], osem.at[i]
                    ).start()

        return carry

    lax.fori_loop(0, (total + 1) // 2, body, 0)

    tail_b[...] = tail[...].astype(BF16)
    for place in range(n):
        pltpu.make_async_copy(tail_b.at[place], scores[place].at[tail_rows], tsem.at[place]).start()

    def finish(i, carry):
        pltpu.make_async_copy(obuf.at[i], scores[0].at[pl.ds(0, TILE)], osem.at[i]).wait()
        return carry

    lax.fori_loop(0, total, finish, 0)
    for place in range(n):
        pltpu.make_async_copy(tail_b.at[place], scores[place].at[tail_rows], tsem.at[place]).wait()


def score_call(
    nz, cap, blk_dev, group, order, runs, fetched, late, resident, me, ids, inv, meta, tiles, local, parts, before, extra
):
    wide = len(group) * cap
    n = len(order)
    items = n * wide
    first_before = 5 + len(runs) + len(parts)
    return pl.pallas_call(
        functools.partial(
            score_kernel, nz, cap, blk_dev, group, order, runs, fetched, late, resident, len(before), len(extra)
        ),
        out_shape=[jax.ShapeDtypeStruct((wide * TILE + (32 if late else 16), BLOCK), BF16)] * n,
        in_specs=[SMEM, SMEM, SMEM, VMEM]
        + [ANY] * (len(runs) + 1)
        + [VMEM if resident else ANY] * len(parts)
        + [ANY] * (len(before) + len(extra)),
        out_specs=[ANY] * n,
        scratch_shapes=[
            pltpu.SMEM((items + 1,), I32),
            pltpu.VMEM((items, TILE, D), BF16),
            pltpu.VMEM((1 if resident else items, BLOCK, D), BF16),
            pltpu.VMEM((items, TILE, BLOCK), BF16),
            pltpu.VMEM((n, 16, BLOCK), F32),
            pltpu.VMEM((n, 16, BLOCK), BF16),
            pltpu.SemaphoreType.DMA((items,)),
            pltpu.SemaphoreType.DMA((items,)),
            pltpu.SemaphoreType.DMA((items,)),
            pltpu.SemaphoreType.DMA((n,)),
        ],
        input_output_aliases={first_before + i: i for i in range(len(before))},
        compiler_params=pltpu.CompilerParams(vmem_limit_bytes=VMEM_BYTES),
        cost_estimate=SHORT,
        name="score",
    )(me, ids, inv, meta, *tiles, local, *parts, *before, *extra)


def assemble_kernel(spans, n_before, n_earlier, inv, *refs):
    n = len(spans)
    sources, before, refs = refs[:n], refs[n : n + n_before], refs[n + n_before + n_earlier :]
    out, primary, picked, held, tail, in_sems, out_sems, tail_sems = refs
    if n_before:
        primary[...] = before[1][...]
        picked[...] = before[2][...]

    def each(act):
        at = 0
        for d, (first, wide) in enumerate(spans):
            for k in range(wide):
                t = inv[first + k]

                @pl.when(t >= 0)
                def _():
                    act(d, k, t, at)

                at += 1

    def tail_copy(d):
        return pltpu.make_async_copy(
            sources[d].at[pl.ds(spans[d][1] * TILE, tail.shape[1])], tail.at[d], tail_sems.at[d]
        )

    def bring(d, k, t, n):
        pltpu.make_async_copy(sources[d].at[pl.ds(k * TILE, TILE)], held.at[n], in_sems.at[n]).start()

    def send(d, k, t, n):
        pltpu.make_async_copy(sources[d].at[pl.ds(k * TILE, TILE)], held.at[n], in_sems.at[n]).wait()
        pltpu.make_async_copy(held.at[n], out.at[t], out_sems.at[n]).start()

    def finish(d, k, t, n):
        pltpu.make_async_copy(held.at[n], out.at[t], out_sems.at[n]).wait()

    for d in range(n):
        tail_copy(d).start()
    each(bring)
    for d in range(n):
        tail_copy(d).wait()
    each(send)
    rows = []
    for d in range(n):
        both = tail[d].astype(F32)
        rows.append(both if both.shape[0] == 16 else both[:16] + both[16:])

    def write(d, k, t, n):
        primary[pl.ds(t, 1), :] = rows[d][k : k + 1, :TILE]
        picked[pl.ds(t, 1), :] = rows[d][k : k + 1, TILE : 2 * TILE]

    each(write)
    each(finish)


def assemble(tile_dev, spans, inv, sources, before, earlier):
    n = len(sources)
    count = sum(wide for _, wide in spans)
    return pl.pallas_call(
        functools.partial(assemble_kernel, spans, len(before), len(earlier)),
        out_shape=[jax.ShapeDtypeStruct((tile_dev, TILE, BLOCK), BF16)]
        + [jax.ShapeDtypeStruct((tile_dev, TILE), F32)] * 2,
        in_specs=[SMEM] + [ANY] * n + [ANY, VMEM, VMEM][: len(before)] + [ANY] * len(earlier),
        out_specs=[ANY, VMEM, VMEM],
        scratch_shapes=[
            pltpu.VMEM((count, TILE, BLOCK), BF16),
            pltpu.VMEM((n, sources[0].shape[0] - spans[0][1] * TILE, BLOCK), BF16),
            pltpu.SemaphoreType.DMA((count,)),
            pltpu.SemaphoreType.DMA((count,)),
            pltpu.SemaphoreType.DMA((n,)),
        ],
        input_output_aliases={1 + n: 0} if before else {},
        compiler_params=pltpu.CompilerParams(vmem_limit_bytes=VMEM_BYTES),
        cost_estimate=SHORT,
        name="assemble",
    )(inv, *sources, *before, *earlier)


def local_part(pieces, vectors, tile_region, tile_block, primary_pick, spill_pick, centers):
    n_parts, n_region, n_shard = (lax.axis_size(a) for a in AXES)
    nz = n_shard // 2
    tile_dev = tile_region.shape[0]
    cap = 2 * tile_dev // (n_region * n_shard)
    slots = nz * cap
    blk_dev = centers.shape[1] // BLOCK
    half_blocks = blk_dev // 2
    pieces = min(pieces, half_blocks)
    sub_blocks = half_blocks // pieces
    shard = lax.axis_index("shard")
    half = lax.axis_index("parts") & 1
    ring, at_ring = ring_place(nz)
    me = jnp.stack(
        [place_of(shard >> 1, nz), shard & 1, lax.axis_index("region"), half]
    ).astype(I32)

    def device(p, r, s):
        return (p * n_region + r) * n_shard + s

    every = [(p, r, s) for p in range(n_parts) for r in range(n_region) for s in range(n_shard)]

    def permute(value, target):
        return lax.ppermute(value, AXES, [(device(*a), device(*target(*a))) for a in every])

    def next_z(p, r, s):
        return (p, r, 2 * ring[(at_ring[s >> 1] + 1) % nz] + (s & 1))

    def other_part(p, r, s):
        return (p ^ 1, r, s)

    local = centers[0].reshape(blk_dev, BLOCK, D)

    def own_piece(i, half):
        return lax.dynamic_slice_in_dim(local, half * half_blocks + i * sub_blocks, sub_blocks, 0)

    own = [own_piece(i, half) for i in range(pieces)]
    tile_rows = vectors.reshape(tile_dev, TILE, D)
    scalars = jnp.pad(jnp.stack([tile_region, tile_block]), ((0, 6), (0, TILE - tile_dev)))
    pack = jnp.concatenate(
        [primary_pick.reshape(tile_dev, TILE), spill_pick.reshape(tile_dev, TILE), scalars]
    )
    at_slot, inv = plan(me, tile_region, tile_block, own, nz, cap, blk_dev)

    def exchange(value, partner):
        if partner == 0:
            return value
        return permute(value, lambda p, r, s: (p, r ^ (partner & 1), s ^ (partner >> 1)))

    packs = [exchange(pack, d) for d in range(4)]
    part = slots // 2
    runs = tuple((d, first, part) for first in (0, part) for d in (2, 3, 1))
    sent = dispatch(at_slot, tile_rows, packs[1:], slots, runs)
    meta, ids = receive(me, packs, nz, cap, blk_dev, tile_dev)

    env, waits, opens = {}, {}, {}

    def across(d):
        return lambda p, r, s: (p, r ^ (d & 1), s ^ (d >> 1))

    steps = (nz - 1) * pieces
    split = sub_blocks // 2 if nz > 2 else 0
    last = steps + 1
    fetched = {}
    starts = {}
    env.update({("z", i + 1 - pieces): own[i] for i in range(pieces)})

    def start(at, name, payload, target, done):
        starts.setdefault(at, []).append((name, payload, target, done))

    for k in range(1, steps + 1):
        hops, first = (k - 1) // pieces + 1, (k - 1) % pieces * sub_blocks
        if split and k == steps:
            start(k - 2, ("z", k), ("z", k - pieces), next_z, None)
            start(k - 1, ("z", last), ("cut", 0), next_z, None)
            start(k - 1, ("x", k), ("cut", 1), other_part, None)
            fetched[hops, True, first, sub_blocks] = ("z", k)
            fetched[hops, False, first, split] = ("x", k)
            fetched[hops, False, first + split, sub_blocks - split] = ("z", last)
        else:
            start(max(0, k - 2), ("z", k), ("z", k - pieces), next_z, k)
            start(k, ("x", k), ("z", k), other_part, k + 1 if k < steps else None)
            fetched[hops, True, first, sub_blocks] = ("z", k)
            fetched[hops, False, first, sub_blocks] = ("x", k)

    times = {0: (0, 2), 1: (0, 3), 2: (5, 6), 3: (2, 4), 4: (3, 5), 5: (5, 6)}
    for i, run in enumerate(runs):
        if run[0] == 1:
            continue
        at, done = (min(g, last - 2 + j) for j, g in enumerate(times[i]))
        env["sent", i] = sent[i]
        if at:
            opens.setdefault(at, []).append(("sent", i))
        start(at, ("t", i), ("sent", i), across(run[0]), done)
    for i, run in enumerate(runs):
        if run[0] == 1:
            env["sent", i] = sent[i]
            opens.setdefault(min(5, last - 1), []).append(("sent", i))
            start(min(5, last - 1), ("t", i), ("sent", i), across(1), None)
    env["t", len(runs)] = tile_rows
    runs += ((0, 0, slots),)

    def score(group, order, late=None, into=False, extra=()):
        resident = into
        keys = tuple(
            key
            for key in fetched
            if key[0] in group and (fetched[key] in (("x", steps), ("z", last))) == resident and fetched[key] in env
        )
        low, high = group[0] * cap, (group[-1] + 1) * cap
        used = [
            i for i, (d, first, count) in enumerate(runs) if d in order and first < high and first + count > low
        ]
        scores = score_call(
            nz, cap, blk_dev, group, order, tuple(runs[i] for i in used), keys, late, resident, me, ids, inv, meta,
            [env["t", i] for i in used], local,
            [env[fetched[key]] for key in keys],
            [env["s", d, group] for d in order] if into else [],
            extra,
        )
        for d, values in zip(order, scores):
            env["s", d, group] = values

    def place(sources, before, earlier=()):
        return assemble(
            tile_dev,
            [(d * slots + group[0] * cap, len(group) * cap) for d, group in sources],
            inv,
            [env["r" if d else "s", d, group] for d, group in sources],
            before,
            earlier,
        )

    one, two, three = (tuple(range(a, b)) for a, b in ((0, nz // 2), (nz // 2, 3 * nz // 4), (3 * nz // 4, nz)))
    plans, at_once = {}, {}
    for ready, order, group, back in (
        (3, (2, 3, 0), one, {2: (4, 5), 3: (5, 6)}),
        (5, (2, 3, 0), two, {2: (0, 6), 3: (6, 7)}),
        (5, (1,), one, {}),
        (5, (1,), two, {}),
    ):
        ready = max(ready, group[-1] * pieces + 1)
        plans.setdefault(ready, []).append((group, order))
        for d, (at, done) in back.items():
            if at:
                at = min(last - 1, max(at, ready + 1))
                opens.setdefault(at, []).append(("s", d, group))
                start(at, ("r", d, group), ("s", d, group), across(d), min(last, max(done, at + 1)))
            else:
                at_once.setdefault(ready, []).append((d, group, min(last, max(done, ready + 1))))
    opens.setdefault(last - 1, []).extend([("s", 1, one), ("s", 1, two)])
    first_late = (pieces - 1) * sub_blocks
    env["token"] = jnp.zeros((8, TILE), F32)
    for k in range(last + 1):
        if k:
            passed = waits.get(k, []) + opens.get(k, [])
            source = ("z", k + 2 - pieces)
            if k + 2 <= steps and k + 2 - pieces < k:
                passed.append(source)
            passed.append("token")
            for name, value in zip(passed, gate([env[n] for n in passed])):
                env[name] = value
        if split and k == steps - 1:
            env["cut", 0] = env["x", steps - pieces][split:]
            env["cut", 1] = env["z", steps][:split]
        for name, payload, target, done in starts.get(k, []):
            env[name] = permute(env[payload], target)
            if done is not None:
                waits.setdefault(done, []).append(name)
        for group, order in plans.get(k, []):
            score(group, order, extra=[env["token"]])
        for d, group, done in at_once.get(k, []):
            env["r", d, group] = exchange(env["s", d, group], d)
            waits.setdefault(done, []).append(("r", d, group))
        if k == last - 1:
            score(three, (2, 3, 1, 0), (first_late, False), extra=[env["token"]])
    score(three, (2, 3, 1, 0), (first_late, True), True, [env["token"]])
    for d in (2, 3, 1):
        env["r", d, three] = exchange(env["s", d, three], d)
    for group in (one, two):
        env["r", 1, group] = exchange(env["s", 1, group], 1)
    outputs = place([(2, one), (3, one), (0, one)], [], [env["s", 0, three]])
    outputs = place([(2, two), (3, two), (0, two), (1, one), (1, two)], outputs, [env["s", 0, three]])
    spill_scores, primary, picked = place([(d, three) for d in (0, 1, 2, 3)], outputs)
    return (
        spill_scores.reshape(tile_dev * TILE, BLOCK),
        primary.astype(BF16).reshape(tile_dev * TILE),
        picked.astype(BF16).reshape(tile_dev * TILE),
    )


def solution(mesh):
    rows = P(AXES, None)
    flat = P(AXES)
    return jax.shard_map(
        functools.partial(local_part, 2),
        mesh=mesh,
        in_specs=(rows, flat, flat, flat, flat, P("region", "shard", None)),
        out_specs=(rows, flat, flat),
        check_vma=False,
    )
```

```python
import functools

import jax
import jax.numpy as jnp
from jax import lax
from jax.experimental import pallas as pl
from jax.experimental.pallas import tpu as pltpu
from jax.sharding import PartitionSpec as P

D = 768
TILE = 128
BLOCK = 512
SMALL_TERM = 1e-05
AXES = ("parts", "region", "shard")
F32 = jnp.float32
BF16 = jnp.bfloat16
I32 = jnp.int32
ANY = pl.BlockSpec(memory_space=pl.ANY)
SMEM = pl.BlockSpec(memory_space=pltpu.SMEM)
SHORT = pl.CostEstimate(flops=1, bytes_accessed=1, transcendentals=0)
VMEM_BYTES = 62 * 1024 * 1024
VMEM = pl.BlockSpec(memory_space=pltpu.VMEM)


def ring_place(nz):
    ring = list(range(0, nz, 2))[:1] + list(range(1, nz, 2)) + list(range(2, nz, 2))[::-1]
    return ring, [ring.index(z) for z in range(nz)]


def place_of(z, nz):
    return jnp.where(z == 0, 0, jnp.where(z & 1 == 1, (z + 1) // 2, nz - z // 2))


def slot_of(nz, cap, blk_dev, at_ring, y, core, region, block):
    shard = block // blk_dev
    partner = 2 * ((shard & 1) ^ y) + (region ^ core)
    cls = lax.rem(at_ring - place_of(shard >> 1, nz) + nz, nz)
    at = partner * nz + cls
    return partner, cls * cap, at


def zero(ref, n):
    def body(i, carry):
        ref[i] = 0
        return carry

    lax.fori_loop(0, n, body, 0)


def plan_kernel(nz, cap, blk_dev, n_before, me, region, block, *refs):
    at_slot, inv, count = refs[n_before:]
    slots = nz * cap

    def clear(i, carry):
        inv[i] = -1
        return carry

    lax.fori_loop(0, 4 * slots, clear, 0)
    zero(count, 4 * nz)

    def place(t, carry):
        partner, first, at = slot_of(nz, cap, blk_dev, me[0], me[1], me[2], region[t], block[t])
        rank = count[at]
        count[at] = rank + 1
        g = partner * slots + first + rank
        inv[g] = t
        at_slot[t] = g
        return carry

    lax.fori_loop(0, region.shape[0], place, 0)


def plan(me, region, block, before, nz, cap, blk_dev):
    return pl.pallas_call(
        functools.partial(plan_kernel, nz, cap, blk_dev, len(before)),
        out_shape=[
            jax.ShapeDtypeStruct(region.shape, I32),
            jax.ShapeDtypeStruct((4 * nz * cap,), I32),
        ],
        in_specs=[SMEM, SMEM, SMEM] + [ANY] * len(before),
        out_specs=[SMEM, SMEM],
        scratch_shapes=[pltpu.SMEM((4 * nz,), I32)],
        compiler_params=pltpu.CompilerParams(vmem_limit_bytes=VMEM_BYTES),
        cost_estimate=SHORT,
        name="plan",
    )(me, region, block, *before)


def receive_kernel(nz, cap, blk_dev, tile_dev, me, *refs):
    packs, (meta, ids, held, scalars, count, held_sems, scalar_sems) = refs[:4], refs[4:]
    slots = nz * cap
    at_ring, y, core = me[0], me[1], me[2]

    def copies(d):
        return (
            pltpu.make_async_copy(packs[d], held.at[d], held_sems.at[d]),
            pltpu.make_async_copy(packs[d].at[pl.ds(2 * tile_dev, 8)], scalars.at[d], scalar_sems.at[d]),
        )

    for d in range(4):
        for copy in copies(d):
            copy.start()

    def clear(i, carry):
        ids[i] = -1
        return carry

    lax.fori_loop(0, 4 * slots, clear, 0)
    for d in range(4):
        for copy in copies(d):
            copy.wait()
        zero(count, 4 * nz)

        def place(t, carry):
            block = scalars[d, 1, t]
            partner, first, at = slot_of(
                nz, cap, blk_dev, at_ring, y ^ (d >> 1), core ^ (d & 1), scalars[d, 0, t], block
            )

            @pl.when(partner == d)
            def _():
                rank = count[at]
                count[at] = rank + 1
                g = d * slots + first + rank
                ids[g] = lax.rem(block, blk_dev)
                meta[g, 1:2, :] = held[d, pl.ds(t, 1), :]
                meta[g, 2:3, :] = held[d, pl.ds(tile_dev + t, 1), :]

            return carry

        lax.fori_loop(0, tile_dev, place, 0)


def receive(me, packs, nz, cap, blk_dev, tile_dev):
    slots = nz * cap
    return pl.pallas_call(
        functools.partial(receive_kernel, nz, cap, blk_dev, tile_dev),
        out_shape=[
            jax.ShapeDtypeStruct((4 * slots, 8, TILE), I32),
            jax.ShapeDtypeStruct((4 * slots,), I32),
        ],
        in_specs=[SMEM] + [ANY] * 4,
        out_specs=[VMEM, SMEM],
        scratch_shapes=[
            pltpu.VMEM((4,) + packs[0].shape, I32),
            pltpu.SMEM((4, 8, TILE), I32),
            pltpu.SMEM((4 * nz,), I32),
            pltpu.SemaphoreType.DMA((4,)),
            pltpu.SemaphoreType.DMA((4,)),
        ],
        compiler_params=pltpu.CompilerParams(vmem_limit_bytes=VMEM_BYTES),
        cost_estimate=SHORT,
        name="receive",
    )(me, *packs)


def dispatch_kernel(slots, runs, n_before, at_slot, vec, *refs):
    refs = refs[n_before:]
    tiles, (held, in_sems, out_sems) = refs[: len(runs)], refs[len(runs) :]
    tile_dev = vec.shape[0]

    def each(act):
        def body(t, carry):
            g = at_slot[t]

            @pl.when(g >= slots)
            def _():
                act(t, g)

            return carry

        lax.fori_loop(0, tile_dev, body, 0)

    def bring(t, g):
        pltpu.make_async_copy(vec.at[t], held.at[t], in_sems.at[t]).start()

    def send(t, g):
        pltpu.make_async_copy(vec.at[t], held.at[t], in_sems.at[t]).wait()
        for ref, (d, first, count) in zip(tiles, runs):
            begin = d * slots + first

            @pl.when((g >= begin) & (g < begin + count))
            def _():
                pltpu.make_async_copy(held.at[t], ref.at[g - begin], out_sems.at[t]).start()

    def finish(t, g):
        pltpu.make_async_copy(held.at[t], tiles[0].at[0], out_sems.at[t]).wait()

    each(bring)
    each(send)
    each(finish)


def dispatch(at_slot, vec, before, slots, runs):
    tile_dev = vec.shape[0]
    return pl.pallas_call(
        functools.partial(dispatch_kernel, slots, runs, len(before)),
        out_shape=[jax.ShapeDtypeStruct((count, TILE, D), BF16) for _, _, count in runs],
        in_specs=[SMEM, ANY] + [ANY] * len(before),
        out_specs=[ANY] * len(runs),
        scratch_shapes=[
            pltpu.VMEM((tile_dev, TILE, D), BF16),
            pltpu.SemaphoreType.DMA((tile_dev,)),
            pltpu.SemaphoreType.DMA((tile_dev,)),
        ],
        compiler_params=pltpu.CompilerParams(vmem_limit_bytes=VMEM_BYTES),
        cost_estimate=SHORT,
        name="dispatch",
    )(at_slot, vec, *before)


def gate_kernel(*refs):
    pass


def gate(passed, others=()):
    n = len(passed)
    return pl.pallas_call(
        gate_kernel,
        out_shape=[jax.ShapeDtypeStruct(v.shape, v.dtype) for v in passed],
        in_specs=[ANY] * n + [VMEM] * len(others),
        out_specs=[ANY] * n,
        input_output_aliases={i: i for i in range(n)},
        compiler_params=pltpu.CompilerParams(vmem_limit_bytes=VMEM_BYTES),
        cost_estimate=SHORT,
        name="gate",
    )(*passed, *others)


def score_math(points, block_rows, meta):
    picks = meta.astype(F32).T.astype(I32)
    lane = lax.broadcasted_iota(I32, (TILE, BLOCK), 1)
    onehot = (lane == picks[:, 1:2]).astype(F32).astype(BF16)
    chosen = jnp.dot(onehot, block_rows, preferred_element_type=F32)
    point_f = points.astype(F32)
    residue = point_f - chosen
    point_sq = jnp.sum(point_f * point_f, axis=1, keepdims=True)
    residue_sq = jnp.sum(residue * residue, axis=1, keepdims=True)
    along = jnp.sum(residue * point_f, axis=1, keepdims=True)
    both = jnp.concatenate([points, residue.astype(BF16)], axis=0)
    products = lax.dot_general(
        both, block_rows, (((1,), (1,)), ((), ())), preferred_element_type=F32
    )
    cross, against = products[:TILE], products[TILE:]
    block_f = block_rows.astype(F32)
    squares = block_f * block_f
    partial = squares[:, :128]
    for k in range(1, D // 128):
        partial = partial + squares[:, k * 128 : (k + 1) * 128]
    center_sq = jnp.sum(partial.T, axis=0, keepdims=True)
    distance = point_sq - 2.0 * cross + center_sq
    mean_sq = residue_sq / D
    off = (along - against) / D
    scores = (distance / D + off * off * (1.0 / (mean_sq + SMALL_TERM))).astype(BF16)
    picked = jnp.sum(
        jnp.where(lane == picks[:, 2:3], scores.astype(F32), 0.0), axis=1, keepdims=True
    )
    column = lax.broadcasted_iota(I32, (TILE, 128), 1)
    small = jnp.where(column == 0, mean_sq, jnp.where(column == 1, picked, 0.0))
    return scores, small.T[:8]


def score_kernel(nz, cap, blk_dev, group, order, runs, fetched, late, resident, aliased, n_extra, me, ids, inv, meta, *refs):
    slots = nz * cap
    wide = len(group) * cap
    n = len(order)
    tiles, refs = refs[: len(runs)], refs[len(runs) :]
    local, parts = refs[0], refs[1 : 1 + len(fetched)]
    refs = refs[1 + len(fetched) + aliased + n_extra :]
    scores = refs[:n]
    work, xbuf, cbuf, obuf, tail, tail_b, xsem, csem, osem, tsem = refs[n:]
    half = me[3]
    half_blocks = blk_dev // 2
    base = group[0] * cap

    total = jnp.int32(0)
    for place, partner in enumerate(order):
        for k in range(wide):
            b = ids[partner * slots + base + k]
            valid = b >= 0
            if late is not None:
                first, wanted = late
                is_late = (b // half_blocks != half) & (b % half_blocks >= first)
                is_late = is_late & (group[k // cap] == nz - 1)
                valid = valid & (is_late == wanted)
            work[total] = place * wide + k
            total = total + valid.astype(I32)

    def start(i):
        code = work[i]
        place = code // wide
        slot = base + code - place * wide
        partner = jnp.int32(order[0])
        for other in range(1, n):
            partner = jnp.where(place == other, order[other], partner)
        b = ids[partner * slots + slot]
        for ref, (d, first, count) in zip(tiles, runs):
            row = slot - first if d else jnp.maximum(inv[slot], 0)

            @pl.when((partner == d) & (slot >= first) & (slot < first + count))
            def _():
                pltpu.make_async_copy(ref.at[row], xbuf.at[i], xsem.at[i]).start()

        cls = slot // cap
        own = b // half_blocks == half
        inside = b % half_blocks

        if resident:
            return

        if group[0] == 0:

            @pl.when(cls == 0)
            def _():
                pltpu.make_async_copy(local.at[b], cbuf.at[i], csem.at[i]).start()

        for ref, (hops, direct, first, count) in zip(parts, fetched):
            right = own if direct else jnp.logical_not(own)

            @pl.when((cls == hops) & right & (inside >= first) & (inside < first + count))
            def _():
                rows = ref.at[inside - first, pl.ds(0, BLOCK)]
                pltpu.make_async_copy(rows, cbuf.at[i], csem.at[i]).start()

    def begin(i, carry):
        start(i)
        return carry

    lax.fori_loop(0, total, begin, 0)
    tail_rows = pl.ds(wide * TILE + 16 * (aliased > 0), 16)
    tail[...] = jnp.zeros(tail.shape, F32)

    def centers_of(i, slot, partner):
        if not resident:
            return cbuf[i]
        inside = ids[partner * slots + slot] % half_blocks
        rows = parts[0][jnp.clip(inside - fetched[0][2], 0, fetched[0][3] - 1)]
        for ref, (hops, direct, first, count) in zip(parts[1:], fetched[1:]):
            rows = jnp.where(inside >= first, ref[jnp.clip(inside - first, 0, count - 1)], rows)
        return rows

    def where(i):
        code = work[i]
        place = code // wide
        partner = jnp.int32(order[0])
        for other in range(1, n):
            partner = jnp.where(place == other, order[other], partner)
        return place, code - place * wide, partner

    def body(pair, carry):
        both = (2 * pair, jnp.minimum(2 * pair + 1, total - 1))
        spots = [where(i) for i in both]
        values = []
        for j, i in enumerate(both):

            @pl.when(2 * pair + j < total)
            def _():
                pltpu.make_async_copy(tiles[0].at[0], xbuf.at[i], xsem.at[i]).wait()
                if not resident:
                    pltpu.make_async_copy(local.at[0], cbuf.at[i], csem.at[i]).wait()

        for i, (place, k, partner) in zip(both, spots):
            rows = centers_of(i, base + k, partner)
            values.append(score_math(xbuf[i], rows, meta[partner * slots + base + k]))
        for i, (place, k, partner), (value, rows) in zip(both, spots, values):
            obuf[i] = value
            tail[place, pl.ds(k, 1), 0 : 2 * TILE] = jnp.concatenate([rows[0:1], rows[1:2]], axis=1)
        for j, (i, (place, k, partner)) in enumerate(zip(both, spots)):
            for other in range(n):

                @pl.when((place == other) & (2 * pair + j < total))
                def _():
                    pltpu.make_async_copy(
                        obuf.at[i], scores[other].at[pl.ds(k * TILE, TILE)], osem.at[i]
                    ).start()

        return carry

    lax.fori_loop(0, (total + 1) // 2, body, 0)

    tail_b[...] = tail[...].astype(BF16)
    for place in range(n):
        pltpu.make_async_copy(tail_b.at[place], scores[place].at[tail_rows], tsem.at[place]).start()

    def finish(i, carry):
        pltpu.make_async_copy(obuf.at[i], scores[0].at[pl.ds(0, TILE)], osem.at[i]).wait()
        return carry

    lax.fori_loop(0, total, finish, 0)
    for place in range(n):
        pltpu.make_async_copy(tail_b.at[place], scores[place].at[tail_rows], tsem.at[place]).wait()


def score_call(
    nz, cap, blk_dev, group, order, runs, fetched, late, resident, me, ids, inv, meta, tiles, local, parts, before, extra
):
    wide = len(group) * cap
    n = len(order)
    items = n * wide
    first_before = 5 + len(runs) + len(parts)
    return pl.pallas_call(
        functools.partial(
            score_kernel, nz, cap, blk_dev, group, order, runs, fetched, late, resident, len(before), len(extra)
        ),
        out_shape=[
            jax.ShapeDtypeStruct((wide * TILE + ((48 if d > 1 else 32) if late else 16), BLOCK), BF16) for d in order
        ],
        in_specs=[SMEM, SMEM, SMEM, VMEM]
        + [ANY] * (len(runs) + 1)
        + [VMEM if resident else ANY] * len(parts)
        + [ANY] * (len(before) + len(extra)),
        out_specs=[ANY] * n,
        scratch_shapes=[
            pltpu.SMEM((items + 1,), I32),
            pltpu.VMEM((items, TILE, D), BF16),
            pltpu.VMEM((1 if resident else items, BLOCK, D), BF16),
            pltpu.VMEM((items, TILE, BLOCK), BF16),
            pltpu.VMEM((n, 16, BLOCK), F32),
            pltpu.VMEM((n, 16, BLOCK), BF16),
            pltpu.SemaphoreType.DMA((items,)),
            pltpu.SemaphoreType.DMA((items,)),
            pltpu.SemaphoreType.DMA((items,)),
            pltpu.SemaphoreType.DMA((n,)),
        ],
        input_output_aliases={first_before + i: i for i in range(len(before))},
        compiler_params=pltpu.CompilerParams(vmem_limit_bytes=VMEM_BYTES),
        cost_estimate=SHORT,
        name="score",
    )(me, ids, inv, meta, *tiles, local, *parts, *before, *extra)


def assemble_kernel(spans, held_already, n_before, n_earlier, last, inv, *refs):
    n = len(spans)
    sources, before, refs = refs[:n], refs[n : n + n_before], refs[n + n_before + n_earlier :]
    out, primary_out, picked_out, primary, picked, held, tail, in_sems, out_sems, tail_sems = refs
    if n_before:
        primary[...] = before[1][...]
        picked[...] = before[2][...]

    def each(act):
        at = 0
        for d, (first, wide) in enumerate(spans):
            for k in range(wide):
                t = inv[first + k]

                @pl.when(t >= 0)
                def _():
                    act(d, pl.ds(k * TILE, TILE), t, at, k)

                at += 1

    def tail_copy(d):
        return pltpu.make_async_copy(
            sources[d].at[pl.ds(spans[d][1] * TILE, tail.shape[1])], tail.at[d], tail_sems.at[d]
        )

    def bring(d, rows, t, at, k):
        if not held_already[d]:
            pltpu.make_async_copy(sources[d].at[rows], held.at[at], in_sems.at[at]).start()

    def send(d, rows, t, at, k):
        if held_already[d]:
            pltpu.make_async_copy(sources[d].at[rows], out.at[t], out_sems.at[at]).start()
        else:
            pltpu.make_async_copy(sources[d].at[rows], held.at[at], in_sems.at[at]).wait()
            pltpu.make_async_copy(held.at[at], out.at[t], out_sems.at[at]).start()

    def finish(d, rows, t, at, k):
        pltpu.make_async_copy(held.at[at], out.at[t], out_sems.at[at]).wait()

    for d in range(n):
        if not held_already[d]:
            tail_copy(d).start()
    each(bring)
    each(send)
    values = []
    for d in range(n):
        if held_already[d]:
            first = spans[d][1] * TILE
            both = sources[d][pl.ds(first, min(32, sources[d].shape[0] - first))].astype(F32)
        else:
            tail_copy(d).wait()
            both = tail[d].astype(F32)
        values.append(both if both.shape[0] == 16 else both[:16] + both[16:])

    def write(d, rows, t, at, k):
        primary[pl.ds(t, 1), :] = values[d][k : k + 1, :TILE]
        picked[pl.ds(t, 1), :] = values[d][k : k + 1, TILE : 2 * TILE]

    each(write)
    primary_out[...] = primary[...].astype(primary_out.dtype)
    picked_out[...] = picked[...].astype(picked_out.dtype)
    each(finish)


def assemble(tile_dev, spans, inv, sources, before, earlier, last):
    n = len(sources)
    count = sum(wide for _, wide in spans)
    tail_rows = 32 if last else 16
    held_already = [last and i > 0 for i in range(n)]
    return pl.pallas_call(
        functools.partial(assemble_kernel, spans, held_already, len(before), len(earlier), last),
        out_shape=[jax.ShapeDtypeStruct((tile_dev, TILE, BLOCK), BF16)]
        + [jax.ShapeDtypeStruct((tile_dev, TILE), BF16 if last else F32)] * 2,
        in_specs=[SMEM]
        + [VMEM if held else ANY for held in held_already]
        + [ANY, VMEM, VMEM][: len(before)]
        + [ANY] * len(earlier),
        out_specs=[ANY, VMEM, VMEM],
        scratch_shapes=[
            pltpu.VMEM((tile_dev, TILE), F32),
            pltpu.VMEM((tile_dev, TILE), F32),
            pltpu.VMEM((count, TILE, BLOCK), BF16),
            pltpu.VMEM((n, tail_rows, BLOCK), BF16),
            pltpu.SemaphoreType.DMA((count,)),
            pltpu.SemaphoreType.DMA((count,)),
            pltpu.SemaphoreType.DMA((n,)),
        ],
        input_output_aliases={1 + n: 0} if before else {},
        compiler_params=pltpu.CompilerParams(vmem_limit_bytes=VMEM_BYTES),
        cost_estimate=SHORT,
        name="assemble",
    )(inv, *sources, *before, *earlier)


def cut_kernel(first, source, target, held, sem):
    rows = pl.ds(0, BLOCK)
    copy = pltpu.make_async_copy(source.at[pl.ds(first, target.shape[0]), rows], held, sem)
    copy.start()
    copy.wait()
    copy = pltpu.make_async_copy(held, target.at[pl.ds(0, target.shape[0]), rows], sem)
    copy.start()
    copy.wait()


def cut(source, first, count, rows=BLOCK):
    return pl.pallas_call(
        functools.partial(cut_kernel, first),
        out_shape=jax.ShapeDtypeStruct((count, rows, D), BF16),
        in_specs=[ANY],
        out_specs=ANY,
        scratch_shapes=[pltpu.VMEM((count, BLOCK, D), BF16), pltpu.SemaphoreType.DMA],
        compiler_params=pltpu.CompilerParams(vmem_limit_bytes=VMEM_BYTES),
        cost_estimate=SHORT,
        name="cut",
    )(source)


def local_part(pieces, vectors, tile_region, tile_block, primary_pick, spill_pick, centers):
    n_parts, n_region, n_shard = (lax.axis_size(a) for a in AXES)
    nz = n_shard // 2
    tile_dev = tile_region.shape[0]
    cap = 2 * tile_dev // (n_region * n_shard)
    slots = nz * cap
    blk_dev = centers.shape[1] // BLOCK
    half_blocks = blk_dev // 2
    pieces = min(pieces, half_blocks)
    sub_blocks = half_blocks // pieces
    shard = lax.axis_index("shard")
    half = lax.axis_index("parts") & 1
    ring, at_ring = ring_place(nz)
    me = jnp.stack(
        [place_of(shard >> 1, nz), shard & 1, lax.axis_index("region"), half]
    ).astype(I32)

    def device(p, r, s):
        return (p * n_region + r) * n_shard + s

    every = [(p, r, s) for p in range(n_parts) for r in range(n_region) for s in range(n_shard)]

    def permute(value, target):
        return lax.ppermute(value, AXES, [(device(*a), device(*target(*a))) for a in every])

    def next_z(p, r, s):
        return (p, r, 2 * ring[(at_ring[s >> 1] + 1) % nz] + (s & 1))

    def other_part(p, r, s):
        return (p ^ 1, r, s)

    local = centers[0].reshape(blk_dev, BLOCK, D)

    def own_piece(i, half):
        return lax.dynamic_slice_in_dim(local, half * half_blocks + i * sub_blocks, sub_blocks, 0)

    own = [own_piece(i, half) for i in range(pieces)]
    tile_rows = vectors.reshape(tile_dev, TILE, D)
    scalars = jnp.pad(jnp.stack([tile_region, tile_block]), ((0, 6), (0, TILE - tile_dev)))
    pack = jnp.concatenate(
        [primary_pick.reshape(tile_dev, TILE), spill_pick.reshape(tile_dev, TILE), scalars]
    )
    at_slot, inv = plan(me, tile_region, tile_block, own, nz, cap, blk_dev)

    def exchange(value, partner):
        if partner == 0:
            return value
        return permute(value, lambda p, r, s: (p, r ^ (partner & 1), s ^ (partner >> 1)))

    packs = [exchange(pack, d) for d in range(4)]
    part = slots // 2
    runs = tuple((d, first, part) for first in (0, part) for d in (2, 3, 1))
    sent = dispatch(at_slot, tile_rows, packs[1:], slots, runs)
    meta, ids = receive(me, packs, nz, cap, blk_dev, tile_dev)

    env, waits, opens = {}, {}, {}

    def across(d):
        return lambda p, r, s: (p, r ^ (d & 1), s ^ (d >> 1))

    steps = (nz - 1) * pieces
    split = sub_blocks // 2 if nz > 2 else 0
    last = steps + 1
    fetched = {}
    starts = {}
    env.update({("z", i + 1 - pieces): own[i] for i in range(pieces)})

    def start(at, name, payload, target, done):
        starts.setdefault(at, []).append((name, payload, target, done))

    for k in range(1, steps + 1):
        hops, first = (k - 1) // pieces + 1, (k - 1) % pieces * sub_blocks
        if split and k == steps:
            start(k - 2, ("z", k), "wide", next_z, None)
            start(k - 1, ("z", last), ("cut", 0), next_z, None)
            fetched[hops, True, first, sub_blocks] = ("z", k)
            fetched[hops, False, first, split] = ("x", k)
            fetched[hops, False, first + split, sub_blocks - split] = ("z", last)
        else:
            start(max(0, k - 2), ("z", k), ("z", k - pieces), next_z, k)
            start(k, ("x", k), ("z", k), other_part, k + 1 if k < steps else None)
            fetched[hops, True, first, sub_blocks] = ("z", k)
            fetched[hops, False, first, sub_blocks] = ("x", k)

    times = {0: (0, 2), 1: (0, 3), 2: (5, 6), 3: (2, 4), 4: (3, 5), 5: (5, 6)}
    for i, run in enumerate(runs):
        if run[0] == 1:
            continue
        at, done = (min(g, last - 2 + j) for j, g in enumerate(times[i]))
        env["sent", i] = sent[i]
        if at:
            opens.setdefault(at, []).append(("sent", i))
        start(at, ("t", i), ("sent", i), across(run[0]), done)
    for i, run in enumerate(runs):
        if run[0] == 1:
            env["sent", i] = sent[i]
            at = last if run[1] else min(5, last - 1)
            opens.setdefault(at, []).append(("sent", i))
            start(at, ("t", i), ("sent", i), across(1), None)
    env["t", len(runs)] = tile_rows
    runs += ((0, 0, slots),)

    def score(group, order, late=None, into=False, extra=()):
        resident = into
        keys = tuple(
            key
            for key in fetched
            if key[0] in group and (late is None or (fetched[key] in (("x", steps), ("z", last))) == resident)
        )
        low, high = group[0] * cap, (group[-1] + 1) * cap
        used = [
            i for i, (d, first, count) in enumerate(runs) if d in order and first < high and first + count > low
        ]
        scores = score_call(
            nz, cap, blk_dev, group, order, tuple(runs[i] for i in used), keys, late, resident, me, ids, inv, meta,
            [env["t", i] for i in used], local,
            [env[fetched[key]] for key in keys],
            [env["s", d, group] for d in order] if into else [],
            extra,
        )
        for d, values in zip(order, scores):
            env["s", d, group] = values

    def place(sources, before, earlier=(), last_call=False):
        return assemble(
            tile_dev,
            [(d * slots + group[0] * cap, len(group) * cap) for d, group in sources],
            inv,
            [env["r" if d else "s", d, group] for d, group in sources],
            before,
            earlier,
            last_call,
        )

    one, two, three = (tuple(range(a, b)) for a, b in ((0, nz // 2), (nz // 2, 3 * nz // 4), (3 * nz // 4, nz)))
    plans, at_once = {}, {}
    for ready, order, group, back in (
        (3, (2, 3, 0), one, {2: (4, 5), 3: (5, 6)}),
        (5, (2, 3, 0), two, {2: (0, 6), 3: (6, 7)}),
        (5, (1,), one, {}),
    ):
        ready = max(ready, group[-1] * pieces + 1)
        plans.setdefault(ready, []).append((group, order))
        for d, (at, done) in back.items():
            if at:
                at = min(last - 1, max(at, ready + 1))
                opens.setdefault(at, []).append(("s", d, group))
                start(at, ("r", d, group), ("s", d, group), across(d), min(last, max(done, at + 1)))
            else:
                at_once.setdefault(ready, []).append((d, group, min(last, max(done, ready + 1))))
    opens.setdefault(last - 1, []).append(("s", 1, one))
    first_late = (pieces - 1) * sub_blocks
    env["token"] = jnp.zeros((8, TILE), F32)
    for k in range(last + 1):
        if k:
            passed = waits.get(k, []) + opens.get(k, [])
            source = ("z", k + 2 - pieces)
            if k + 2 <= steps and k + 2 - pieces < k:
                passed.append(source)
            passed.append("token")
            others = [env["x", steps], env["z", last]] if split and k == last else []
            for name, value in zip(passed, gate([env[n] for n in passed], others)):
                env[name] = value
        if split and k == steps - 2:
            env["wide"] = cut(env["z", k], 0, sub_blocks, rows=BLOCK + 16)
        if split and k == steps - 1:
            env["cut", 0] = cut(env["x", steps - pieces], split, sub_blocks - split)
        for name, payload, target, done in starts.get(k, []):
            env[name] = permute(env[payload], target)
            if done is not None:
                waits.setdefault(done, []).append(name)
        for group, order in plans.get(k, []):
            score(group, order, extra=[env["token"]])
        if split and k == steps - 1:
            env["x", steps] = permute(cut(env["z", steps], 0, split), other_part)
        for d, group, done in at_once.get(k, []):
            env["r", d, group] = exchange(env["s", d, group], d)
            waits.setdefault(done, []).append(("r", d, group))
        if k == last - 1:
            score(three, (2, 3, 0), (first_late, False), extra=[env["token"]])
    score(three, (2, 3), (first_late, True), True, [env["token"]])
    for d in (2, 3):
        env["r", d, three] = exchange(env["s", d, three], d)
    score(three, (0,), (first_late, True), True, [env["s", 2, three]])
    for group in (two, three):
        score(group, (1,), extra=[env["s", 2, three]])
    for group in (one, two, three):
        env["r", 1, group] = exchange(env["s", 1, group], 1)
    outputs = place([(0, one), (2, one), (3, one)], [], [env["s", 0, three]])
    outputs = place([(0, two), (2, two), (3, two), (1, one), (1, two)], outputs, [env["s", 0, three]])
    spill_scores, primary, picked = place([(d, three) for d in (0, 1, 2, 3)], outputs, last_call=True)
    return (
        spill_scores.reshape(tile_dev * TILE, BLOCK),
        primary.reshape(tile_dev * TILE),
        picked.reshape(tile_dev * TILE),
    )


def solution(mesh):
    rows = P(AXES, None)
    flat = P(AXES)
    return jax.shard_map(
        functools.partial(local_part, 2),
        mesh=mesh,
        in_specs=(rows, flat, flat, flat, flat, P("region", "shard", None)),
        out_specs=(rows, flat, flat),
        check_vma=False,
    )
```

```python
import functools

import jax
import jax.numpy as jnp
from jax import lax
from jax.experimental import pallas as pl
from jax.experimental.pallas import tpu as pltpu
from jax.sharding import PartitionSpec as P

D = 768
TILE = 128
BLOCK = 512
SMALL_TERM = 1e-05
AXES = ("parts", "region", "shard")
F32 = jnp.float32
BF16 = jnp.bfloat16
I32 = jnp.int32
ANY = pl.BlockSpec(memory_space=pl.ANY)
SMEM = pl.BlockSpec(memory_space=pltpu.SMEM)
SHORT = pl.CostEstimate(flops=1, bytes_accessed=1, transcendentals=0)
VMEM_BYTES = 63 * 1024 * 1024 + 512 * 1024
VMEM_LESS = 60 * 1024 * 1024
VMEM = pl.BlockSpec(memory_space=pltpu.VMEM)


def ring_place(nz):
    ring = list(range(0, nz, 2))[:1] + list(range(1, nz, 2)) + list(range(2, nz, 2))[::-1]
    return ring, [ring.index(z) for z in range(nz)]


def place_of(z, nz):
    return jnp.where(z == 0, 0, jnp.where(z & 1 == 1, (z + 1) // 2, nz - z // 2))


def slot_of(nz, cap, blk_dev, at_ring, y, core, region, block):
    shard = block // blk_dev
    partner = 2 * ((shard & 1) ^ y) + (region ^ core)
    cls = lax.rem(at_ring - place_of(shard >> 1, nz) + nz, nz)
    at = partner * nz + cls
    return partner, cls * cap, at


def zero(ref, n):
    def body(i, carry):
        ref[i] = 0
        return carry

    lax.fori_loop(0, n, body, 0)


def plan_kernel(nz, cap, blk_dev, n_before, me, region, block, *refs):
    at_slot, inv, count = refs[n_before:]
    slots = nz * cap

    def clear(i, carry):
        inv[i] = -1
        return carry

    lax.fori_loop(0, 4 * slots, clear, 0)
    zero(count, 4 * nz)

    def place(t, carry):
        partner, first, at = slot_of(nz, cap, blk_dev, me[0], me[1], me[2], region[t], block[t])
        rank = count[at]
        count[at] = rank + 1
        g = partner * slots + first + rank
        inv[g] = t
        at_slot[t] = g
        return carry

    lax.fori_loop(0, region.shape[0], place, 0)


def plan(me, region, block, before, nz, cap, blk_dev):
    return pl.pallas_call(
        functools.partial(plan_kernel, nz, cap, blk_dev, len(before)),
        out_shape=[
            jax.ShapeDtypeStruct(region.shape, I32),
            jax.ShapeDtypeStruct((4 * nz * cap,), I32),
        ],
        in_specs=[SMEM, SMEM, SMEM] + [ANY] * len(before),
        out_specs=[SMEM, SMEM],
        scratch_shapes=[pltpu.SMEM((4 * nz,), I32)],
        compiler_params=pltpu.CompilerParams(vmem_limit_bytes=VMEM_BYTES),
        cost_estimate=SHORT,
        name="plan",
    )(me, region, block, *before)


def receive_kernel(nz, cap, blk_dev, tile_dev, me, *refs):
    packs, (meta, ids, held, scalars, count, held_sems, scalar_sems) = refs[:4], refs[4:]
    slots = nz * cap
    at_ring, y, core = me[0], me[1], me[2]

    def copies(d):
        return (
            pltpu.make_async_copy(packs[d], held.at[d], held_sems.at[d]),
            pltpu.make_async_copy(packs[d].at[pl.ds(2 * tile_dev, 8)], scalars.at[d], scalar_sems.at[d]),
        )

    for d in range(4):
        for copy in copies(d):
            copy.start()

    def clear(i, carry):
        ids[i] = -1
        return carry

    lax.fori_loop(0, 4 * slots, clear, 0)
    for d in range(4):
        for copy in copies(d):
            copy.wait()
        zero(count, 4 * nz)

        def place(t, carry):
            block = scalars[d, 1, t]
            partner, first, at = slot_of(
                nz, cap, blk_dev, at_ring, y ^ (d >> 1), core ^ (d & 1), scalars[d, 0, t], block
            )

            @pl.when(partner == d)
            def _():
                rank = count[at]
                count[at] = rank + 1
                g = d * slots + first + rank
                ids[g] = lax.rem(block, blk_dev)
                meta[g, 1:2, :] = held[d, pl.ds(t, 1), :]
                meta[g, 2:3, :] = held[d, pl.ds(tile_dev + t, 1), :]

            return carry

        lax.fori_loop(0, tile_dev, place, 0)


def receive(me, packs, nz, cap, blk_dev, tile_dev):
    slots = nz * cap
    return pl.pallas_call(
        functools.partial(receive_kernel, nz, cap, blk_dev, tile_dev),
        out_shape=[
            jax.ShapeDtypeStruct((4 * slots, 8, TILE), I32),
            jax.ShapeDtypeStruct((4 * slots,), I32),
        ],
        in_specs=[SMEM] + [ANY] * 4,
        out_specs=[VMEM, SMEM],
        scratch_shapes=[
            pltpu.VMEM((4,) + packs[0].shape, I32),
            pltpu.SMEM((4, 8, TILE), I32),
            pltpu.SMEM((4 * nz,), I32),
            pltpu.SemaphoreType.DMA((4,)),
            pltpu.SemaphoreType.DMA((4,)),
        ],
        compiler_params=pltpu.CompilerParams(vmem_limit_bytes=VMEM_BYTES),
        cost_estimate=SHORT,
        name="receive",
    )(me, *packs)


def dispatch_kernel(slots, runs, n_before, at_slot, vec, *refs):
    refs = refs[n_before:]
    tiles, (held, in_sems, out_sems) = refs[: len(runs)], refs[len(runs) :]
    tile_dev = vec.shape[0]

    def each(act):
        def body(t, carry):
            g = at_slot[t]

            @pl.when(g >= slots)
            def _():
                act(t, g)

            return carry

        lax.fori_loop(0, tile_dev, body, 0)

    def bring(t, g):
        pltpu.make_async_copy(vec.at[t], held.at[t], in_sems.at[t]).start()

    def send(t, g):
        pltpu.make_async_copy(vec.at[t], held.at[t], in_sems.at[t]).wait()
        for ref, (d, first, count) in zip(tiles, runs):
            begin = d * slots + first

            @pl.when((g >= begin) & (g < begin + count))
            def _():
                pltpu.make_async_copy(held.at[t], ref.at[g - begin], out_sems.at[t]).start()

    def finish(t, g):
        pltpu.make_async_copy(held.at[t], tiles[0].at[0], out_sems.at[t]).wait()

    each(bring)
    each(send)
    each(finish)


def dispatch(at_slot, vec, before, slots, runs):
    tile_dev = vec.shape[0]
    return pl.pallas_call(
        functools.partial(dispatch_kernel, slots, runs, len(before)),
        out_shape=[jax.ShapeDtypeStruct((count, TILE, D), BF16) for _, _, count in runs],
        in_specs=[SMEM, ANY] + [ANY] * len(before),
        out_specs=[ANY] * len(runs),
        scratch_shapes=[
            pltpu.VMEM((tile_dev, TILE, D), BF16),
            pltpu.SemaphoreType.DMA((tile_dev,)),
            pltpu.SemaphoreType.DMA((tile_dev,)),
        ],
        compiler_params=pltpu.CompilerParams(vmem_limit_bytes=VMEM_BYTES),
        cost_estimate=SHORT,
        name="dispatch",
    )(at_slot, vec, *before)


def gate_kernel(*refs):
    pass


def gate(passed, others=()):
    n = len(passed)
    return pl.pallas_call(
        gate_kernel,
        out_shape=[jax.ShapeDtypeStruct(v.shape, v.dtype) for v in passed],
        in_specs=[ANY] * (n + len(others)),
        out_specs=[ANY] * n,
        input_output_aliases={i: i for i in range(n)},
        compiler_params=pltpu.CompilerParams(vmem_limit_bytes=VMEM_BYTES),
        cost_estimate=SHORT,
        name="gate",
    )(*passed, *others)


def score_math(points, block_rows, meta):
    picks = meta.astype(F32).T.astype(I32)
    lane = lax.broadcasted_iota(I32, (TILE, BLOCK), 1)
    onehot = (lane == picks[:, 1:2]).astype(F32).astype(BF16)
    chosen = jnp.dot(onehot, block_rows, preferred_element_type=F32)
    point_f = points.astype(F32)
    residue = point_f - chosen
    point_sq = jnp.sum(point_f * point_f, axis=1, keepdims=True)
    residue_sq = jnp.sum(residue * residue, axis=1, keepdims=True)
    along = jnp.sum(residue * point_f, axis=1, keepdims=True)
    both = jnp.concatenate([points, residue.astype(BF16)], axis=0)
    products = lax.dot_general(
        both, block_rows, (((1,), (1,)), ((), ())), preferred_element_type=F32
    )
    cross, against = products[:TILE], products[TILE:]
    block_f = block_rows.astype(F32)
    squares = block_f * block_f
    partial = squares[:, :128]
    for k in range(1, D // 128):
        partial = partial + squares[:, k * 128 : (k + 1) * 128]
    center_sq = jnp.sum(partial.T, axis=0, keepdims=True)
    distance = point_sq - 2.0 * cross + center_sq
    mean_sq = residue_sq / D
    off = (along - against) / D
    scores = (distance / D + off * off * (1.0 / (mean_sq + SMALL_TERM))).astype(BF16)
    picked = jnp.sum(
        jnp.where(lane == picks[:, 2:3], scores.astype(F32), 0.0), axis=1, keepdims=True
    )
    column = lax.broadcasted_iota(I32, (TILE, 128), 1)
    small = jnp.where(column == 0, mean_sq, jnp.where(column == 1, picked, 0.0))
    return scores, small.T[:8]


def score_kernel(nz, cap, blk_dev, places, wide, runs, fetched, late, resident, aliased, n_extra, me, ids, inv, meta, *refs):
    slots = nz * cap
    n = len(places)
    tiles, refs = refs[: len(runs)], refs[len(runs) :]
    local, parts = refs[0], refs[1 : 1 + len(fetched)]
    refs = refs[1 + len(fetched) + aliased + n_extra :]
    scores = refs[:n]
    work, xbuf, cbuf, obuf, tail, tail_b, xsem, csem, osem, tsem = refs[n:]
    half = me[3]
    half_blocks = blk_dev // 2

    total = jnp.int32(0)
    for place, (partner, base) in enumerate(places):
        for k in range(wide):
            b = ids[partner * slots + base + k]
            valid = b >= 0
            if late is not None:
                first, wanted = late
                is_late = (b // half_blocks != half) & (b % half_blocks >= first)
                is_late = is_late & ((base + k) // cap == nz - 1)
                valid = valid & (is_late == wanted)
            work[total] = place * wide + k
            total = total + valid.astype(I32)

    def where(i):
        code = work[i]
        place = code // wide
        partner, base = jnp.int32(places[0][0]), jnp.int32(places[0][1])
        for other in range(1, n):
            partner = jnp.where(place == other, places[other][0], partner)
            base = jnp.where(place == other, places[other][1], base)
        k = code - place * wide
        return place, k, partner, base + k

    def start(i):
        place, k, partner, slot = where(i)
        b = ids[partner * slots + slot]
        for ref, (d, first, count) in zip(tiles, runs):
            row = slot - first if d else jnp.maximum(inv[slot], 0)

            @pl.when((partner == d) & (slot >= first) & (slot < first + count))
            def _():
                pltpu.make_async_copy(ref.at[row], xbuf.at[i], xsem.at[i]).start()

        cls = slot // cap
        own = b // half_blocks == half
        inside = b % half_blocks

        if resident:
            return

        if any(base == 0 for _, base in places):

            @pl.when(cls == 0)
            def _():
                pltpu.make_async_copy(local.at[b], cbuf.at[i], csem.at[i]).start()

        for ref, (hops, direct, first, count) in zip(parts, fetched):
            right = own if direct else jnp.logical_not(own)

            @pl.when((cls == hops) & right & (inside >= first) & (inside < first + count))
            def _():
                rows = ref.at[inside - first, pl.ds(0, BLOCK)]
                pltpu.make_async_copy(rows, cbuf.at[i], csem.at[i]).start()

    def begin(i, carry):
        start(i)
        return carry

    def whole_parts():
        at = 0
        for p, (ref, (hops, direct, first, count)) in enumerate(zip(parts, fetched)):
            yield pltpu.make_async_copy(ref, cbuf.at[pl.ds(at, count)], csem.at[p])
            at += count

    if resident:
        for copy in whole_parts():
            copy.start()
    lax.fori_loop(0, total, begin, 0)
    tail_rows = pl.ds(wide * TILE + 16 * (aliased > 0), 16)
    tail[...] = jnp.zeros(tail.shape, F32)

    def centers_of(i, slot, partner):
        if not resident:
            return cbuf[i]
        inside = ids[partner * slots + slot] % half_blocks
        row, at = jnp.int32(0), 0
        for hops, direct, first, count in fetched:
            row = jnp.where((inside >= first) & (inside < first + count), at + inside - first, row)
            at += count
        return cbuf[row]

    def body(pair, carry):
        both = (2 * pair, jnp.minimum(2 * pair + 1, total - 1))
        spots = [where(i) for i in both]
        values = []
        for j, i in enumerate(both):

            @pl.when(2 * pair + j < total)
            def _():
                pltpu.make_async_copy(tiles[0].at[0], xbuf.at[i], xsem.at[i]).wait()
                if not resident:
                    pltpu.make_async_copy(local.at[0], cbuf.at[i], csem.at[i]).wait()

        for i, (place, k, partner, slot) in zip(both, spots):
            rows = centers_of(i, slot, partner)
            values.append(score_math(xbuf[i], rows, meta[partner * slots + slot]))
        for i, (place, k, _, _), (value, rows) in zip(both, spots, values):
            obuf[i] = value
            tail[place, pl.ds(k, 1), 0 : 2 * TILE] = jnp.concatenate([rows[0:1], rows[1:2]], axis=1)
        for j, (i, (place, k, _, _)) in enumerate(zip(both, spots)):
            for other in range(n):

                @pl.when((place == other) & (2 * pair + j < total))
                def _():
                    pltpu.make_async_copy(
                        obuf.at[i], scores[other].at[pl.ds(k * TILE, TILE)], osem.at[i]
                    ).start()

        return carry

    if resident:
        for copy in whole_parts():
            copy.wait()
    lax.fori_loop(0, (total + 1) // 2, body, 0)

    tail_b[...] = tail[...].astype(BF16)
    for place in range(n):
        pltpu.make_async_copy(tail_b.at[place], scores[place].at[tail_rows], tsem.at[place]).start()

    def finish(i, carry):
        pltpu.make_async_copy(obuf.at[i], scores[0].at[pl.ds(0, TILE)], osem.at[i]).wait()
        return carry

    lax.fori_loop(0, total, finish, 0)
    for place in range(n):
        pltpu.make_async_copy(tail_b.at[place], scores[place].at[tail_rows], tsem.at[place]).wait()


def score_call(
    nz, cap, blk_dev, places, wide, runs, fetched, late, resident, me, ids, inv, meta, tiles, local, parts, before, extra
):
    n = len(places)
    items = n * wide
    first_before = 5 + len(runs) + len(parts)
    return pl.pallas_call(
        functools.partial(
            score_kernel, nz, cap, blk_dev, places, wide, runs, fetched, late, resident, len(before), len(extra)
        ),
        out_shape=[
            jax.ShapeDtypeStruct((wide * TILE + (32 if late else 16), BLOCK), BF16) for d, _ in places
        ],
        in_specs=[SMEM, SMEM, SMEM, VMEM]
        + [ANY] * (len(runs) + 1)
        + [ANY] * (len(parts) + len(before) + len(extra)),
        out_specs=[ANY] * n,
        scratch_shapes=[
            pltpu.SMEM((items + 1,), I32),
            pltpu.VMEM((items, TILE, D), BF16),
            pltpu.VMEM((sum(key[3] for key in fetched) if resident else items, BLOCK, D), BF16),
            pltpu.VMEM((items, TILE, BLOCK), BF16),
            pltpu.VMEM((n, 16, BLOCK), F32),
            pltpu.VMEM((n, 16, BLOCK), BF16),
            pltpu.SemaphoreType.DMA((items,)),
            pltpu.SemaphoreType.DMA((items,)),
            pltpu.SemaphoreType.DMA((items,)),
            pltpu.SemaphoreType.DMA((n,)),
        ],
        input_output_aliases={first_before + i: i for i in range(len(before))},
        compiler_params=pltpu.CompilerParams(vmem_limit_bytes=VMEM_BYTES),
        cost_estimate=SHORT,
        name="score",
    )(me, ids, inv, meta, *tiles, local, *parts, *before, *extra)


def assemble_kernel(spans, held_already, n_before, n_earlier, last, inv, *refs):
    n = len(spans)
    sources, before, refs = refs[:n], refs[n : n + n_before], refs[n + n_before + n_earlier :]
    out, primary_out, picked_out, primary, picked, held, tail, in_sems, out_sems, tail_sems = refs
    if n_before:
        primary[...] = before[1][...]
        picked[...] = before[2][...]

    def each(act):
        at = 0
        for d, (first, wide) in enumerate(spans):
            for k in range(wide):
                t = inv[first + k]

                @pl.when(t >= 0)
                def _():
                    act(d, pl.ds(k * TILE, TILE), t, at, k)

                at += 1

    def tail_copy(d):
        return pltpu.make_async_copy(
            sources[d].at[pl.ds(spans[d][1] * TILE, tail.shape[1])], tail.at[d], tail_sems.at[d]
        )

    def bring(d, rows, t, at, k):
        if not held_already[d]:
            pltpu.make_async_copy(sources[d].at[rows], held.at[at], in_sems.at[at]).start()

    def send(d, rows, t, at, k):
        if held_already[d]:
            pltpu.make_async_copy(sources[d].at[rows], out.at[t], out_sems.at[at]).start()
        else:
            pltpu.make_async_copy(sources[d].at[rows], held.at[at], in_sems.at[at]).wait()
            pltpu.make_async_copy(held.at[at], out.at[t], out_sems.at[at]).start()

    def finish(d, rows, t, at, k):
        pltpu.make_async_copy(held.at[at], out.at[t], out_sems.at[at]).wait()

    for d in range(n):
        if not held_already[d]:
            tail_copy(d).start()
    each(bring)
    each(send)
    values = []
    for d in range(n):
        if held_already[d]:
            first = spans[d][1] * TILE
            both = sources[d][pl.ds(first, min(32, sources[d].shape[0] - first))].astype(F32)
        else:
            tail_copy(d).wait()
            both = tail[d].astype(F32)
        values.append(both if both.shape[0] == 16 else both[:16] + both[16:])

    def write(d, rows, t, at, k):
        primary[pl.ds(t, 1), :] = values[d][k : k + 1, :TILE]
        picked[pl.ds(t, 1), :] = values[d][k : k + 1, TILE : 2 * TILE]

    each(write)
    primary_out[...] = primary[...].astype(primary_out.dtype)
    picked_out[...] = picked[...].astype(picked_out.dtype)
    each(finish)


def assemble(tile_dev, spans, inv, sources, before, earlier, last):
    n = len(sources)
    count = sum(wide for _, wide in spans)
    tail_rows = 32 if last else 16
    held_already = [last and i > 0 for i in range(n)]
    return pl.pallas_call(
        functools.partial(assemble_kernel, spans, held_already, len(before), len(earlier), last),
        out_shape=[jax.ShapeDtypeStruct((tile_dev, TILE, BLOCK), BF16)]
        + [jax.ShapeDtypeStruct((tile_dev, TILE), BF16 if last else F32)] * 2,
        in_specs=[SMEM]
        + [VMEM if held else ANY for held in held_already]
        + [ANY, VMEM, VMEM][: len(before)]
        + [ANY] * len(earlier),
        out_specs=[ANY, VMEM, VMEM],
        scratch_shapes=[
            pltpu.VMEM((tile_dev, TILE), F32),
            pltpu.VMEM((tile_dev, TILE), F32),
            pltpu.VMEM((count, TILE, BLOCK), BF16),
            pltpu.VMEM((n, tail_rows, BLOCK), BF16),
            pltpu.SemaphoreType.DMA((count,)),
            pltpu.SemaphoreType.DMA((count,)),
            pltpu.SemaphoreType.DMA((n,)),
        ],
        input_output_aliases={1 + n: 0} if before else {},
        compiler_params=pltpu.CompilerParams(vmem_limit_bytes=VMEM_LESS if last else VMEM_BYTES),
        cost_estimate=SHORT,
        name="assemble",
    )(inv, *sources, *before, *earlier)


def cut_kernel(first, source, target, held, sem):
    rows = pl.ds(0, BLOCK)
    copy = pltpu.make_async_copy(source.at[pl.ds(first, target.shape[0]), rows], held, sem)
    copy.start()
    copy.wait()
    copy = pltpu.make_async_copy(held, target.at[pl.ds(0, target.shape[0]), rows], sem)
    copy.start()
    copy.wait()


def cut(source, first, count, rows=BLOCK):
    return pl.pallas_call(
        functools.partial(cut_kernel, first),
        out_shape=jax.ShapeDtypeStruct((count, rows, D), BF16),
        in_specs=[ANY],
        out_specs=ANY,
        scratch_shapes=[pltpu.VMEM((count, BLOCK, D), BF16), pltpu.SemaphoreType.DMA],
        compiler_params=pltpu.CompilerParams(vmem_limit_bytes=VMEM_BYTES),
        cost_estimate=SHORT,
        name="cut",
    )(source)


def local_part(pieces, vectors, tile_region, tile_block, primary_pick, spill_pick, centers):
    n_parts, n_region, n_shard = (lax.axis_size(a) for a in AXES)
    nz = n_shard // 2
    tile_dev = tile_region.shape[0]
    cap = 2 * tile_dev // (n_region * n_shard)
    slots = nz * cap
    blk_dev = centers.shape[1] // BLOCK
    half_blocks = blk_dev // 2
    pieces = min(pieces, half_blocks)
    sub_blocks = half_blocks // pieces
    shard = lax.axis_index("shard")
    half = lax.axis_index("parts") & 1
    ring, at_ring = ring_place(nz)
    me = jnp.stack(
        [place_of(shard >> 1, nz), shard & 1, lax.axis_index("region"), half]
    ).astype(I32)

    def device(p, r, s):
        return (p * n_region + r) * n_shard + s

    every = [(p, r, s) for p in range(n_parts) for r in range(n_region) for s in range(n_shard)]

    def permute(value, target):
        return lax.ppermute(value, AXES, [(device(*a), device(*target(*a))) for a in every])

    def next_z(p, r, s):
        return (p, r, 2 * ring[(at_ring[s >> 1] + 1) % nz] + (s & 1))

    def other_part(p, r, s):
        return (p ^ 1, r, s)

    local = centers[0].reshape(blk_dev, BLOCK, D)

    def own_piece(i, half):
        return lax.dynamic_slice_in_dim(local, half * half_blocks + i * sub_blocks, sub_blocks, 0)

    own = [own_piece(i, half) for i in range(pieces)]
    tile_rows = vectors.reshape(tile_dev, TILE, D)
    scalars = jnp.pad(jnp.stack([tile_region, tile_block]), ((0, 6), (0, TILE - tile_dev)))
    pack = jnp.concatenate(
        [primary_pick.reshape(tile_dev, TILE), spill_pick.reshape(tile_dev, TILE), scalars]
    )
    at_slot, inv = plan(me, tile_region, tile_block, own, nz, cap, blk_dev)

    def exchange(value, partner):
        if partner == 0:
            return value
        return permute(value, lambda p, r, s: (p, r ^ (partner & 1), s ^ (partner >> 1)))

    packs = [exchange(pack, d) for d in range(4)]
    part = slots // 2
    runs = tuple((d, first, part) for first in (0, part) for d in (2, 3, 1))
    sent = dispatch(at_slot, tile_rows, packs[1:], slots, runs)
    meta, ids = receive(me, packs, nz, cap, blk_dev, tile_dev)

    env, waits, opens = {}, {}, {}

    def across(d):
        return lambda p, r, s: (p, r ^ (d & 1), s ^ (d >> 1))

    steps = (nz - 1) * pieces
    split = sub_blocks // 2 if nz > 2 else 0
    last = steps + 1
    fetched = {}
    starts = {}
    env.update({("z", i + 1 - pieces): own[i] for i in range(pieces)})

    def start(at, name, payload, target, done):
        starts.setdefault(at, []).append((name, payload, target, done))

    for k in range(1, steps + 1):
        hops, first = (k - 1) // pieces + 1, (k - 1) % pieces * sub_blocks
        if split and k == steps:
            start(k - 2, ("z", k), "wide", next_z, None)
            start(k - 1, ("z", last), ("cut", 0), next_z, None)
            fetched[hops, True, first, sub_blocks] = ("z", k)
            fetched[hops, False, first, split] = ("x", k)
            fetched[hops, False, first + split, sub_blocks - split] = ("z", last)
        else:
            start(max(0, k - 2), ("z", k), ("z", k - pieces), next_z, k)
            start(k, ("x", k), ("z", k), other_part, k + 1 if k < steps else None)
            fetched[hops, True, first, sub_blocks] = ("z", k)
            fetched[hops, False, first, sub_blocks] = ("x", k)

    times = {0: (0, 2), 1: (0, 3), 2: (5, 6), 3: (2, 4), 4: (3, 5), 5: (5, 6)}
    for i, run in enumerate(runs):
        if run[0] == 1:
            continue
        at, done = (min(g, last - 2 + j) for j, g in enumerate(times[i]))
        env["sent", i] = sent[i]
        if at:
            opens.setdefault(at, []).append(("sent", i))
        start(at, ("t", i), ("sent", i), across(run[0]), done)
    for i, run in enumerate(runs):
        if run[0] == 1:
            env["sent", i] = sent[i]
            at = last if run[1] else min(5, last - 1)
            opens.setdefault(at, []).append(("sent", i))
            start(at, ("t", i), ("sent", i), across(1), None)
    env["t", len(runs)] = tile_rows
    runs += ((0, 0, slots),)

    def score(where, late=None, into=False, extra=()):
        resident = into
        keys = tuple(
            key
            for key in fetched
            if any(key[0] in group for _, group in where)
            and (late is None or (fetched[key] in (("x", steps), ("z", last))) == resident)
        )
        wide = len(where[0][1]) * cap
        places = tuple((d, group[0] * cap) for d, group in where)
        used = [
            i
            for i, (d, first, count) in enumerate(runs)
            if any(d == partner and first < base + wide and first + count > base for partner, base in places)
        ]
        scores = score_call(
            nz, cap, blk_dev, places, wide, tuple(runs[i] for i in used), keys, late, resident, me, ids, inv, meta,
            [env["t", i] for i in used], local,
            [env[fetched[key]] for key in keys],
            [env["s", d, group] for d, group in where] if into else [],
            extra,
        )
        for (d, group), values in zip(where, scores):
            env["s", d, group] = values

    def place(sources, before, earlier=(), last_call=False):
        return assemble(
            tile_dev,
            [(d * slots + group[0] * cap, len(group) * cap) for d, group in sources],
            inv,
            [env["r" if d else "s", d, group] for d, group in sources],
            before,
            earlier,
            last_call,
        )

    one, two, three = (tuple(range(a, b)) for a, b in ((0, nz // 2), (nz // 2, 3 * nz // 4), (3 * nz // 4, nz)))
    plans, at_once = {}, {}
    for ready, order, group, back in (
        (3, (2, 3, 0), one, {2: (4, 5), 3: (5, 6)}),
        (5, (2, 3, 0), two, {2: (0, 6), 3: (6, 7)}),
        (5, (1,), one, {}),
    ):
        ready = max(ready, group[-1] * pieces + 1)
        plans.setdefault(ready, []).append((group, order))
        for d, (at, done) in back.items():
            if at:
                at = min(last - 1, max(at, ready + 1))
                opens.setdefault(at, []).append(("s", d, group))
                start(at, ("r", d, group), ("s", d, group), across(d), min(last, max(done, at + 1)))
            else:
                at_once.setdefault(ready, []).append((d, group, min(last, max(done, ready + 1))))
    opens.setdefault(last - 1, []).append(("s", 1, one))
    first_late = (pieces - 1) * sub_blocks
    env["token"] = jnp.zeros((8, TILE), F32)
    for k in range(last + 1):
        if k:
            passed = waits.get(k, []) + opens.get(k, [])
            source = ("z", k + 2 - pieces)
            if k + 2 <= steps and k + 2 - pieces < k:
                passed.append(source)
            passed.append("token")
            others = [env["x", steps], env["z", last]] if split and k == last else []
            for name, value in zip(passed, gate([env[n] for n in passed], others)):
                env[name] = value
        if split and k == steps - 2:
            env["wide"] = cut(env["z", k], 0, sub_blocks, rows=BLOCK + 16)
        if split and k == steps - 1:
            env["cut", 0] = cut(env["x", steps - pieces], split, sub_blocks - split)
        for name, payload, target, done in starts.get(k, []):
            env[name] = permute(env[payload], target)
            if done is not None:
                waits.setdefault(done, []).append(name)
        for group, order in plans.get(k, []):
            score([(d, group) for d in order], extra=[env["token"]])
        if split and k == steps - 1:
            env["x", steps] = permute(cut(env["z", steps], 0, split), other_part)
        for d, group, done in at_once.get(k, []):
            env["r", d, group] = exchange(env["s", d, group], d)
            waits.setdefault(done, []).append(("r", d, group))
        if k == last - 1:
            score([(d, three) for d in (2, 3, 0)], (first_late, False), extra=[env["token"]])
    score([(2, three), (3, three)], (first_late, True), True, [env["token"]])
    for d in (2, 3):
        env["r", d, three] = exchange(env["s", d, three], d)
    score([(0, three)], (first_late, True), True, [env["s", 2, three]])
    score([(1, two), (1, three)], extra=[env["s", 2, three]])
    for group in (one, two, three):
        env["r", 1, group] = exchange(env["s", 1, group], 1)
    outputs = place([(0, one), (2, one), (3, one)], [], [env["s", 2, three]])
    outputs = place([(0, two), (2, two), (3, two), (1, one), (1, two)], outputs, [env["s", 0, three]])
    spill_scores, primary, picked = place([(d, three) for d in (0, 1, 2, 3)], outputs, last_call=True)
    return (
        spill_scores.reshape(tile_dev * TILE, BLOCK),
        primary.reshape(tile_dev * TILE),
        picked.reshape(tile_dev * TILE),
    )


def solution(mesh):
    rows = P(AXES, None)
    flat = P(AXES)
    return jax.shard_map(
        functools.partial(local_part, 2),
        mesh=mesh,
        in_specs=(rows, flat, flat, flat, flat, P("region", "shard", None)),
        out_specs=(rows, flat, flat),
        check_vma=False,
    )
```

```python
import functools

import jax
import jax.numpy as jnp
from jax import lax
from jax.experimental import pallas as pl
from jax.experimental.pallas import tpu as pltpu
from jax.sharding import PartitionSpec as P

D = 768
TILE = 128
BLOCK = 512
SMALL_TERM = 1e-05
AXES = ("parts", "region", "shard")
F32 = jnp.float32
BF16 = jnp.bfloat16
I32 = jnp.int32
ANY = pl.BlockSpec(memory_space=pl.ANY)
SMEM = pl.BlockSpec(memory_space=pltpu.SMEM)
SHORT = pl.CostEstimate(flops=1, bytes_accessed=1, transcendentals=0)
VMEM_BYTES = 63 * 1024 * 1024 + 512 * 1024
VMEM_LESS = 60 * 1024 * 1024
VMEM = pl.BlockSpec(memory_space=pltpu.VMEM)


def ring_place(nz):
    ring = list(range(0, nz, 2))[:1] + list(range(1, nz, 2)) + list(range(2, nz, 2))[::-1]
    return ring, [ring.index(z) for z in range(nz)]


def place_of(z, nz):
    return jnp.where(z == 0, 0, jnp.where(z & 1 == 1, (z + 1) // 2, nz - z // 2))


def slot_of(nz, cap, blk_dev, at_ring, y, core, region, block):
    shard = block // blk_dev
    partner = 2 * ((shard & 1) ^ y) + (region ^ core)
    cls = lax.rem(at_ring - place_of(shard >> 1, nz) + nz, nz)
    at = partner * nz + cls
    return partner, cls * cap, at


def zero(ref, n):
    def body(i, carry):
        ref[i] = 0
        return carry

    lax.fori_loop(0, n, body, 0)


def plan_kernel(nz, cap, blk_dev, n_before, me, region, block, *refs):
    at_slot, inv, token, count = refs[n_before:]
    slots = nz * cap
    token[...] = jnp.zeros(token.shape, F32)

    def clear(i, carry):
        inv[i] = -1
        return carry

    lax.fori_loop(0, 4 * slots, clear, 0)
    zero(count, 4 * nz)

    def place(t, carry):
        partner, first, at = slot_of(nz, cap, blk_dev, me[0], me[1], me[2], region[t], block[t])
        rank = count[at]
        count[at] = rank + 1
        g = partner * slots + first + rank
        inv[g] = t
        at_slot[t] = g
        return carry

    lax.fori_loop(0, region.shape[0], place, 0)


def plan(me, region, block, before, nz, cap, blk_dev):
    return pl.pallas_call(
        functools.partial(plan_kernel, nz, cap, blk_dev, len(before)),
        out_shape=[
            jax.ShapeDtypeStruct(region.shape, I32),
            jax.ShapeDtypeStruct((4 * nz * cap,), I32),
            jax.ShapeDtypeStruct((8, TILE), F32),
        ],
        in_specs=[SMEM, SMEM, SMEM] + [ANY] * len(before),
        out_specs=[SMEM, SMEM, VMEM],
        scratch_shapes=[pltpu.SMEM((4 * nz,), I32)],
        compiler_params=pltpu.CompilerParams(vmem_limit_bytes=VMEM_BYTES),
        cost_estimate=SHORT,
        name="plan",
    )(me, region, block, *before)


def receive_kernel(nz, cap, blk_dev, tile_dev, me, *refs):
    packs, (meta, ids, held, scalars, count, held_sems, scalar_sems) = refs[:4], refs[4:]
    slots = nz * cap
    at_ring, y, core = me[0], me[1], me[2]

    def copies(d):
        return (
            pltpu.make_async_copy(packs[d], held.at[d], held_sems.at[d]),
            pltpu.make_async_copy(packs[d].at[pl.ds(2 * tile_dev, 8)], scalars.at[d], scalar_sems.at[d]),
        )

    for d in range(4):
        for copy in copies(d):
            copy.start()

    def clear(i, carry):
        ids[i] = -1
        return carry

    lax.fori_loop(0, 4 * slots, clear, 0)
    for d in range(4):
        for copy in copies(d):
            copy.wait()
        zero(count, 4 * nz)

        def place(t, carry):
            block = scalars[d, 1, t]
            partner, first, at = slot_of(
                nz, cap, blk_dev, at_ring, y ^ (d >> 1), core ^ (d & 1), scalars[d, 0, t], block
            )

            @pl.when(partner == d)
            def _():
                rank = count[at]
                count[at] = rank + 1
                g = d * slots + first + rank
                ids[g] = lax.rem(block, blk_dev)
                meta[g, 1:2, :] = held[d, pl.ds(t, 1), :]
                meta[g, 2:3, :] = held[d, pl.ds(tile_dev + t, 1), :]

            return carry

        lax.fori_loop(0, tile_dev, place, 0)


def receive(me, packs, nz, cap, blk_dev, tile_dev):
    slots = nz * cap
    return pl.pallas_call(
        functools.partial(receive_kernel, nz, cap, blk_dev, tile_dev),
        out_shape=[
            jax.ShapeDtypeStruct((4 * slots, 8, TILE), I32),
            jax.ShapeDtypeStruct((4 * slots,), I32),
        ],
        in_specs=[SMEM] + [ANY] * 4,
        out_specs=[VMEM, SMEM],
        scratch_shapes=[
            pltpu.VMEM((4,) + packs[0].shape, I32),
            pltpu.SMEM((4, 8, TILE), I32),
            pltpu.SMEM((4 * nz,), I32),
            pltpu.SemaphoreType.DMA((4,)),
            pltpu.SemaphoreType.DMA((4,)),
        ],
        compiler_params=pltpu.CompilerParams(vmem_limit_bytes=VMEM_BYTES),
        cost_estimate=SHORT,
        name="receive",
    )(me, *packs)


def dispatch_kernel(slots, runs, n_before, at_slot, vec, *refs):
    refs = refs[n_before:]
    tiles, (held, in_sems, out_sems) = refs[: len(runs)], refs[len(runs) :]
    tile_dev = vec.shape[0]

    def each(act):
        def body(t, carry):
            g = at_slot[t]

            @pl.when(g >= slots)
            def _():
                act(t, g)

            return carry

        lax.fori_loop(0, tile_dev, body, 0)

    def bring(t, g):
        pltpu.make_async_copy(vec.at[t], held.at[t], in_sems.at[t]).start()

    def send(t, g):
        pltpu.make_async_copy(vec.at[t], held.at[t], in_sems.at[t]).wait()
        for ref, (d, first, count) in zip(tiles, runs):
            begin = d * slots + first

            @pl.when((g >= begin) & (g < begin + count))
            def _():
                pltpu.make_async_copy(held.at[t], ref.at[g - begin], out_sems.at[t]).start()

    def finish(t, g):
        pltpu.make_async_copy(held.at[t], tiles[0].at[0], out_sems.at[t]).wait()

    each(bring)
    each(send)
    each(finish)


def dispatch(at_slot, vec, before, slots, runs):
    tile_dev = vec.shape[0]
    return pl.pallas_call(
        functools.partial(dispatch_kernel, slots, runs, len(before)),
        out_shape=[jax.ShapeDtypeStruct((count, TILE, D), BF16) for _, _, count in runs],
        in_specs=[SMEM, ANY] + [ANY] * len(before),
        out_specs=[ANY] * len(runs),
        scratch_shapes=[
            pltpu.VMEM((tile_dev, TILE, D), BF16),
            pltpu.SemaphoreType.DMA((tile_dev,)),
            pltpu.SemaphoreType.DMA((tile_dev,)),
        ],
        compiler_params=pltpu.CompilerParams(vmem_limit_bytes=VMEM_BYTES),
        cost_estimate=SHORT,
        name="dispatch",
    )(at_slot, vec, *before)


def gate_kernel(*refs):
    pass


def gate(passed, others=()):
    n = len(passed)
    return pl.pallas_call(
        gate_kernel,
        out_shape=[jax.ShapeDtypeStruct(v.shape, v.dtype) for v in passed],
        in_specs=[ANY] * (n + len(others)),
        out_specs=[ANY] * n,
        input_output_aliases={i: i for i in range(n)},
        compiler_params=pltpu.CompilerParams(vmem_limit_bytes=VMEM_BYTES),
        cost_estimate=SHORT,
        name="gate",
    )(*passed, *others)


def score_math(points, block_rows, meta):
    picks = meta.astype(F32).T.astype(I32)
    lane = lax.broadcasted_iota(I32, (TILE, BLOCK), 1)
    onehot = (lane == picks[:, 1:2]).astype(F32).astype(BF16)
    chosen = jnp.dot(onehot, block_rows, preferred_element_type=F32)
    point_f = points.astype(F32)
    residue = point_f - chosen
    point_sq = jnp.sum(point_f * point_f, axis=1, keepdims=True)
    residue_sq = jnp.sum(residue * residue, axis=1, keepdims=True)
    along = jnp.sum(residue * point_f, axis=1, keepdims=True)
    both = jnp.concatenate([points, residue.astype(BF16)], axis=0)
    products = lax.dot_general(
        both, block_rows, (((1,), (1,)), ((), ())), preferred_element_type=F32
    )
    cross, against = products[:TILE], products[TILE:]
    block_f = block_rows.astype(F32)
    squares = block_f * block_f
    partial = squares[:, :128]
    for k in range(1, D // 128):
        partial = partial + squares[:, k * 128 : (k + 1) * 128]
    center_sq = jnp.sum(partial.T, axis=0, keepdims=True)
    distance = point_sq - 2.0 * cross + center_sq
    mean_sq = residue_sq / D
    off = (along - against) / D
    scores = (distance / D + off * off * (1.0 / (mean_sq + SMALL_TERM))).astype(BF16)
    picked = jnp.sum(
        jnp.where(lane == picks[:, 2:3], scores.astype(F32), 0.0), axis=1, keepdims=True
    )
    column = lax.broadcasted_iota(I32, (TILE, 128), 1)
    small = jnp.where(column == 0, mean_sq, jnp.where(column == 1, picked, 0.0))
    return scores, small.T[:8]


def score_kernel(nz, cap, blk_dev, places, wide, runs, fetched, late, resident, aliased, n_extra, me, ids, inv, meta, *refs):
    slots = nz * cap
    n = len(places)
    tiles, refs = refs[: len(runs)], refs[len(runs) :]
    local, parts = refs[0], refs[1 : 1 + len(fetched)]
    refs = refs[1 + len(fetched) + aliased + n_extra :]
    scores = refs[:n]
    work, xbuf, cbuf, obuf, tail, tail_b, xsem, csem, osem, tsem = refs[n:]
    half = me[3]
    half_blocks = blk_dev // 2

    total = jnp.int32(0)
    for place, (partner, base) in enumerate(places):
        for k in range(wide):
            b = ids[partner * slots + base + k]
            valid = b >= 0
            if late is not None:
                first, wanted = late
                is_late = (b // half_blocks != half) & (b % half_blocks >= first)
                is_late = is_late & ((base + k) // cap == nz - 1)
                valid = valid & (is_late == wanted)
            work[total] = place * wide + k
            total = total + valid.astype(I32)

    def where(i):
        code = work[i]
        place = code // wide
        partner, base = jnp.int32(places[0][0]), jnp.int32(places[0][1])
        for other in range(1, n):
            partner = jnp.where(place == other, places[other][0], partner)
            base = jnp.where(place == other, places[other][1], base)
        k = code - place * wide
        return place, k, partner, base + k

    def start(i):
        place, k, partner, slot = where(i)
        b = ids[partner * slots + slot]
        for ref, (d, first, count) in zip(tiles, runs):
            row = slot - first if d else jnp.maximum(inv[slot], 0)

            @pl.when((partner == d) & (slot >= first) & (slot < first + count))
            def _():
                pltpu.make_async_copy(ref.at[row], xbuf.at[i], xsem.at[i]).start()

        cls = slot // cap
        own = b // half_blocks == half
        inside = b % half_blocks

        if resident:
            return

        if any(base == 0 for _, base in places):

            @pl.when(cls == 0)
            def _():
                pltpu.make_async_copy(local.at[b], cbuf.at[i], csem.at[i]).start()

        for ref, (hops, direct, first, count) in zip(parts, fetched):
            right = own if direct else jnp.logical_not(own)

            @pl.when((cls == hops) & right & (inside >= first) & (inside < first + count))
            def _():
                rows = ref.at[inside - first, pl.ds(0, BLOCK)]
                pltpu.make_async_copy(rows, cbuf.at[i], csem.at[i]).start()

    def begin(i, carry):
        start(i)
        return carry

    def whole_parts():
        at = 0
        for p, (ref, (hops, direct, first, count)) in enumerate(zip(parts, fetched)):
            yield pltpu.make_async_copy(ref, cbuf.at[pl.ds(at, count)], csem.at[p])
            at += count

    if resident:
        for copy in whole_parts():
            copy.start()
    lax.fori_loop(0, total, begin, 0)
    tail_rows = pl.ds(wide * TILE + 16 * (aliased > 0), 16)
    tail[...] = jnp.zeros(tail.shape, F32)

    def centers_of(i, slot, partner):
        if not resident:
            return cbuf[i]
        inside = ids[partner * slots + slot] % half_blocks
        row, at = jnp.int32(0), 0
        for hops, direct, first, count in fetched:
            row = jnp.where((inside >= first) & (inside < first + count), at + inside - first, row)
            at += count
        return cbuf[row]

    def body(pair, carry):
        both = (2 * pair, jnp.minimum(2 * pair + 1, total - 1))
        spots = [where(i) for i in both]
        values = []
        for j, i in enumerate(both):

            @pl.when(2 * pair + j < total)
            def _():
                pltpu.make_async_copy(tiles[0].at[0], xbuf.at[i], xsem.at[i]).wait()
                if not resident:
                    pltpu.make_async_copy(local.at[0], cbuf.at[i], csem.at[i]).wait()

        for i, (place, k, partner, slot) in zip(both, spots):
            rows = centers_of(i, slot, partner)
            values.append(score_math(xbuf[i], rows, meta[partner * slots + slot]))
        for i, (place, k, _, _), (value, rows) in zip(both, spots, values):
            obuf[i] = value
            tail[place, pl.ds(k, 1), 0 : 2 * TILE] = jnp.concatenate([rows[0:1], rows[1:2]], axis=1)
        for j, (i, (place, k, _, _)) in enumerate(zip(both, spots)):
            for other in range(n):

                @pl.when((place == other) & (2 * pair + j < total))
                def _():
                    pltpu.make_async_copy(
                        obuf.at[i], scores[other].at[pl.ds(k * TILE, TILE)], osem.at[i]
                    ).start()

        return carry

    if resident:
        for copy in whole_parts():
            copy.wait()
    lax.fori_loop(0, (total + 1) // 2, body, 0)

    tail_b[...] = tail[...].astype(BF16)
    for place in range(n):
        pltpu.make_async_copy(tail_b.at[place], scores[place].at[tail_rows], tsem.at[place]).start()

    def finish(i, carry):
        pltpu.make_async_copy(obuf.at[i], scores[0].at[pl.ds(0, TILE)], osem.at[i]).wait()
        return carry

    lax.fori_loop(0, total, finish, 0)
    for place in range(n):
        pltpu.make_async_copy(tail_b.at[place], scores[place].at[tail_rows], tsem.at[place]).wait()


def score_call(
    nz, cap, blk_dev, places, wide, runs, fetched, late, resident, me, ids, inv, meta, tiles, local, parts, before, extra
):
    n = len(places)
    items = n * wide
    first_before = 5 + len(runs) + len(parts)
    return pl.pallas_call(
        functools.partial(
            score_kernel, nz, cap, blk_dev, places, wide, runs, fetched, late, resident, len(before), len(extra)
        ),
        out_shape=[
            jax.ShapeDtypeStruct((wide * TILE + (32 if late else 16), BLOCK), BF16) for d, _ in places
        ],
        in_specs=[SMEM, SMEM, SMEM, VMEM]
        + [ANY] * (len(runs) + 1)
        + [ANY] * (len(parts) + len(before) + len(extra)),
        out_specs=[ANY] * n,
        scratch_shapes=[
            pltpu.SMEM((items + 1,), I32),
            pltpu.VMEM((items, TILE, D), BF16),
            pltpu.VMEM((sum(key[3] for key in fetched) if resident else items, BLOCK, D), BF16),
            pltpu.VMEM((items, TILE, BLOCK), BF16),
            pltpu.VMEM((n, 16, BLOCK), F32),
            pltpu.VMEM((n, 16, BLOCK), BF16),
            pltpu.SemaphoreType.DMA((items,)),
            pltpu.SemaphoreType.DMA((items,)),
            pltpu.SemaphoreType.DMA((items,)),
            pltpu.SemaphoreType.DMA((n,)),
        ],
        input_output_aliases={first_before + i: i for i in range(len(before))},
        compiler_params=pltpu.CompilerParams(vmem_limit_bytes=VMEM_BYTES),
        cost_estimate=SHORT,
        name="score",
    )(me, ids, inv, meta, *tiles, local, *parts, *before, *extra)


def assemble_kernel(spans, held_already, n_before, n_earlier, last, inv, *refs):
    n = len(spans)
    sources, before, refs = refs[:n], refs[n : n + n_before], refs[n + n_before + n_earlier :]
    out, primary_out, picked_out, primary, picked, held, tail, in_sems, out_sems, tail_sems = refs
    if n_before:
        primary[...] = before[1][...]
        picked[...] = before[2][...]

    def each(act):
        at = 0
        for d, (first, wide) in enumerate(spans):
            for k in range(wide):
                t = inv[first + k]

                @pl.when(t >= 0)
                def _():
                    act(d, pl.ds(k * TILE, TILE), t, at, k)

                at += 1

    def tail_rows(d):
        return sources[d].shape[0] - spans[d][1] * TILE

    def tail_copy(d):
        return pltpu.make_async_copy(
            sources[d].at[pl.ds(spans[d][1] * TILE, tail_rows(d))], tail.at[d, pl.ds(0, tail_rows(d))], tail_sems.at[d]
        )

    def bring(d, rows, t, at, k):
        if not held_already[d]:
            pltpu.make_async_copy(sources[d].at[rows], held.at[at], in_sems.at[at]).start()

    def send(d, rows, t, at, k):
        if held_already[d]:
            pltpu.make_async_copy(sources[d].at[rows], out.at[t], out_sems.at[at]).start()
        else:
            pltpu.make_async_copy(sources[d].at[rows], held.at[at], in_sems.at[at]).wait()
            pltpu.make_async_copy(held.at[at], out.at[t], out_sems.at[at]).start()

    def finish(d, rows, t, at, k):
        pltpu.make_async_copy(held.at[at], out.at[t], out_sems.at[at]).wait()

    for d in range(n):
        if not held_already[d]:
            tail_copy(d).start()
    each(bring)
    each(send)
    values = []
    for d in range(n):
        if held_already[d]:
            both = sources[d][pl.ds(spans[d][1] * TILE, tail_rows(d))].astype(F32)
        else:
            tail_copy(d).wait()
            both = tail[d, pl.ds(0, tail_rows(d))].astype(F32)
        values.append(both if both.shape[0] == 16 else both[:16] + both[16:])

    def write(d, rows, t, at, k):
        primary[pl.ds(t, 1), :] = values[d][k : k + 1, :TILE]
        picked[pl.ds(t, 1), :] = values[d][k : k + 1, TILE : 2 * TILE]

    each(write)
    primary_out[...] = primary[...].astype(primary_out.dtype)
    picked_out[...] = picked[...].astype(picked_out.dtype)
    each(finish)


def assemble(tile_dev, spans, inv, sources, before, earlier, last):
    n = len(sources)
    count = sum(wide for _, wide in spans)
    tail_rows = 32 if last else 16
    held_already = [last and i > 0 for i in range(n)]
    return pl.pallas_call(
        functools.partial(assemble_kernel, spans, held_already, len(before), len(earlier), last),
        out_shape=[jax.ShapeDtypeStruct((tile_dev, TILE, BLOCK), BF16)]
        + [jax.ShapeDtypeStruct((tile_dev, TILE), BF16 if last else F32)] * 2,
        in_specs=[SMEM]
        + [VMEM if held else ANY for held in held_already]
        + [ANY, VMEM, VMEM][: len(before)]
        + [ANY] * len(earlier),
        out_specs=[ANY, VMEM, VMEM],
        scratch_shapes=[
            pltpu.VMEM((tile_dev, TILE), F32),
            pltpu.VMEM((tile_dev, TILE), F32),
            pltpu.VMEM((count, TILE, BLOCK), BF16),
            pltpu.VMEM((n, tail_rows, BLOCK), BF16),
            pltpu.SemaphoreType.DMA((count,)),
            pltpu.SemaphoreType.DMA((count,)),
            pltpu.SemaphoreType.DMA((n,)),
        ],
        input_output_aliases={1 + n: 0} if before else {},
        compiler_params=pltpu.CompilerParams(vmem_limit_bytes=VMEM_LESS if last else VMEM_BYTES),
        cost_estimate=SHORT,
        name="assemble",
    )(inv, *sources, *before, *earlier)


def cut_kernel(first, source, target, held, in_sems, out_sems):
    step = BLOCK // 4
    runs = [(i, pl.ds(j * step, step)) for i in range(target.shape[0]) for j in range(4)]
    brought = [
        pltpu.make_async_copy(source.at[first + i, rows], held.at[i, rows], in_sems.at[n])
        for n, (i, rows) in enumerate(runs)
    ]
    sent = [
        pltpu.make_async_copy(held.at[i, rows], target.at[i, rows], out_sems.at[n])
        for n, (i, rows) in enumerate(runs)
    ]
    for copy in brought:
        copy.start()
    for arrived, copy in zip(brought, sent):
        arrived.wait()
        copy.start()
    for copy in sent:
        copy.wait()


def own_kernel(blocks, source, *refs):
    pieces, (held, in_sems, out_sems) = refs[:-3], refs[-3:]
    total = blocks * len(pieces)
    first = (lax.axis_index("parts") & 1) * total
    brought = [
        pltpu.make_async_copy(source.at[first + i], held.at[i], in_sems.at[i]) for i in range(total)
    ]
    sent = [
        pltpu.make_async_copy(held.at[i], pieces[i // blocks].at[i % blocks], out_sems.at[i]) for i in range(total)
    ]
    for copy in brought:
        copy.start()
    for arrived, copy in zip(brought, sent):
        arrived.wait()
        copy.start()
    for copy in sent:
        copy.wait()


def own_pieces(source, pieces, blocks):
    total = pieces * blocks
    return pl.pallas_call(
        functools.partial(own_kernel, blocks),
        out_shape=[jax.ShapeDtypeStruct((blocks, BLOCK, D), BF16)] * pieces,
        in_specs=[ANY],
        out_specs=[ANY] * pieces,
        scratch_shapes=[
            pltpu.VMEM((total, BLOCK, D), BF16),
            pltpu.SemaphoreType.DMA((total,)),
            pltpu.SemaphoreType.DMA((total,)),
        ],
        compiler_params=pltpu.CompilerParams(vmem_limit_bytes=VMEM_BYTES),
        cost_estimate=SHORT,
        name="own_pieces",
    )(source)


def cut(source, first, count, rows=BLOCK):
    return pl.pallas_call(
        functools.partial(cut_kernel, first),
        out_shape=jax.ShapeDtypeStruct((count, rows, D), BF16),
        in_specs=[ANY],
        out_specs=ANY,
        scratch_shapes=[
            pltpu.VMEM((count, BLOCK, D), BF16),
            pltpu.SemaphoreType.DMA((4 * count,)),
            pltpu.SemaphoreType.DMA((4 * count,)),
        ],
        compiler_params=pltpu.CompilerParams(vmem_limit_bytes=VMEM_BYTES),
        cost_estimate=SHORT,
        name="cut",
    )(source)


def local_part(pieces, vectors, tile_region, tile_block, primary_pick, spill_pick, centers):
    n_parts, n_region, n_shard = (lax.axis_size(a) for a in AXES)
    nz = n_shard // 2
    tile_dev = tile_region.shape[0]
    cap = 2 * tile_dev // (n_region * n_shard)
    slots = nz * cap
    blk_dev = centers.shape[1] // BLOCK
    half_blocks = blk_dev // 2
    pieces = min(pieces, half_blocks)
    sub_blocks = half_blocks // pieces
    shard = lax.axis_index("shard")
    half = lax.axis_index("parts") & 1
    ring, at_ring = ring_place(nz)
    me = jnp.stack(
        [place_of(shard >> 1, nz), shard & 1, lax.axis_index("region"), half]
    ).astype(I32)

    def device(p, r, s):
        return (p * n_region + r) * n_shard + s

    every = [(p, r, s) for p in range(n_parts) for r in range(n_region) for s in range(n_shard)]

    def permute(value, target):
        return lax.ppermute(value, AXES, [(device(*a), device(*target(*a))) for a in every])

    def next_z(p, r, s):
        return (p, r, 2 * ring[(at_ring[s >> 1] + 1) % nz] + (s & 1))

    def other_part(p, r, s):
        return (p ^ 1, r, s)

    local = centers[0].reshape(blk_dev, BLOCK, D)

    own = own_pieces(local, pieces, sub_blocks)
    tile_rows = vectors.reshape(tile_dev, TILE, D)
    scalars = jnp.pad(jnp.stack([tile_region, tile_block]), ((0, 6), (0, TILE - tile_dev)))
    pack = jnp.concatenate(
        [primary_pick.reshape(tile_dev, TILE), spill_pick.reshape(tile_dev, TILE), scalars]
    )
    at_slot, inv, token = plan(me, tile_region, tile_block, own, nz, cap, blk_dev)

    def exchange(value, partner):
        if partner == 0:
            return value
        return permute(value, lambda p, r, s: (p, r ^ (partner & 1), s ^ (partner >> 1)))

    packs = [exchange(pack, d) for d in range(4)]
    part = slots // 2
    runs = tuple((d, first, part) for first in (0, part) for d in (2, 3, 1))
    sent = dispatch(at_slot, tile_rows, packs[1:], slots, runs)
    meta, ids = receive(me, packs, nz, cap, blk_dev, tile_dev)

    env, waits, opens = {}, {}, {}

    def across(d):
        return lambda p, r, s: (p, r ^ (d & 1), s ^ (d >> 1))

    steps = (nz - 1) * pieces
    split = sub_blocks // 2 if nz > 2 else 0
    last = steps + 1
    fetched = {}
    starts = {}
    env.update({("z", i + 1 - pieces): own[i] for i in range(pieces)})

    def start(at, name, payload, target, done):
        starts.setdefault(at, []).append((name, payload, target, done))

    for k in range(1, steps + 1):
        hops, first = (k - 1) // pieces + 1, (k - 1) % pieces * sub_blocks
        if split and k == steps:
            start(k - 2, ("z", k), "wide", next_z, None)
            start(k - 1, ("z", last), ("cut", 0), next_z, None)
            fetched[hops, True, first, sub_blocks] = ("z", k)
            fetched[hops, False, first, split] = ("x", k)
            fetched[hops, False, first + split, sub_blocks - split] = ("z", last)
        else:
            start(max(0, k - 2), ("z", k), ("z", k - pieces), next_z, k)
            start(k, ("x", k), ("z", k), other_part, k + 1 if k < steps else None)
            fetched[hops, True, first, sub_blocks] = ("z", k)
            fetched[hops, False, first, sub_blocks] = ("x", k)

    times = {0: (0, 2), 1: (0, 3), 2: (5, 6), 3: (2, 4), 4: (3, 5), 5: (5, 6)}
    for i, run in enumerate(runs):
        if run[0] == 1:
            continue
        at, done = (min(g, last - 2 + j) for j, g in enumerate(times[i]))
        env["sent", i] = sent[i]
        if at:
            opens.setdefault(at, []).append(("sent", i))
        start(at, ("t", i), ("sent", i), across(run[0]), done)
    for i, run in enumerate(runs):
        if run[0] == 1:
            env["sent", i] = sent[i]
            at = last if run[1] else min(5, last - 1)
            opens.setdefault(at, []).append(("sent", i))
            start(at, ("t", i), ("sent", i), across(1), None)
    env["t", len(runs)] = tile_rows
    runs += ((0, 0, slots),)

    def score(where, late=None, into=False, extra=()):
        resident = into
        keys = tuple(
            key
            for key in fetched
            if any(key[0] in group for _, group in where)
            and (late is None or (fetched[key] in (("x", steps), ("z", last))) == resident)
        )
        wide = len(where[0][1]) * cap
        places = tuple((d, group[0] * cap) for d, group in where)
        used = [
            i
            for i, (d, first, count) in enumerate(runs)
            if any(d == partner and first < base + wide and first + count > base for partner, base in places)
        ]
        scores = score_call(
            nz, cap, blk_dev, places, wide, tuple(runs[i] for i in used), keys, late, resident, me, ids, inv, meta,
            [env["t", i] for i in used], local,
            [env[fetched[key]] for key in keys],
            [env["s", d, group] for d, group in where] if into else [],
            extra,
        )
        for (d, group), values in zip(where, scores):
            env["s", d, group] = values

    def place(sources, before, earlier=(), last_call=False):
        return assemble(
            tile_dev,
            [(d * slots + group[0] * cap, len(group) * cap) for d, group in sources],
            inv,
            [env["r" if d else "s", d, group] for d, group in sources],
            before,
            earlier,
            last_call,
        )

    one, two, three = (tuple(range(a, b)) for a, b in ((0, nz // 2), (nz // 2, 3 * nz // 4), (3 * nz // 4, nz)))
    plans, at_once = {}, {}
    for ready, order, group, back in (
        (3, (2, 3, 0), one, {2: (4, 5), 3: (5, 6)}),
        (5, (2, 3, 0), two, {2: (0, 6), 3: (6, 7)}),
        (5, (1,), one, {}),
    ):
        ready = max(ready, group[-1] * pieces + 1)
        plans.setdefault(ready, []).append((group, order))
        for d, (at, done) in back.items():
            if at:
                at = min(last - 1, max(at, ready + 1))
                opens.setdefault(at, []).append(("s", d, group))
                start(at, ("r", d, group), ("s", d, group), across(d), min(last, max(done, at + 1)))
            else:
                at_once.setdefault(ready, []).append((d, group, min(last, max(done, ready + 1))))
    opens.setdefault(last - 1, []).append(("s", 1, one))
    first_late = (pieces - 1) * sub_blocks
    env["token"] = token
    for k in range(last + 1):
        if k:
            passed = waits.get(k, []) + opens.get(k, [])
            source = ("z", k + 2 - pieces)
            if k + 2 <= steps and k + 2 - pieces < k:
                passed.append(source)
            passed.append("token")
            others = [env["x", steps], env["z", last]] if split and k == last else []
            for name, value in zip(passed, gate([env[n] for n in passed], others)):
                env[name] = value
        if split and k == steps - 2:
            env["wide"] = cut(env["z", k], 0, sub_blocks, rows=BLOCK + 16)
        if split and k == steps - 1:
            env["cut", 0] = cut(env["x", steps - pieces], split, sub_blocks - split)
        for name, payload, target, done in starts.get(k, []):
            env[name] = permute(env[payload], target)
            if done is not None:
                waits.setdefault(done, []).append(name)
        for group, order in plans.get(k, []):
            score([(d, group) for d in order], extra=[env["token"]])
        if split and k == steps - 1:
            env["x", steps] = permute(cut(env["z", steps], 0, split), other_part)
        for d, group, done in at_once.get(k, []):
            env["r", d, group] = exchange(env["s", d, group], d)
            waits.setdefault(done, []).append(("r", d, group))
        if k == last - 1:
            score([(d, three) for d in (2, 3)], (first_late, False), extra=[env["token"]])
    score([(2, three), (3, three)], (first_late, True), True, [env["token"]])
    for d in (2, 3):
        env["r", d, three] = exchange(env["s", d, three], d)
    score([(1, two), (1, three), (0, three)], extra=[env["s", 2, three]])
    for group in (one, two, three):
        env["r", 1, group] = exchange(env["s", 1, group], 1)
    outputs = place([(0, one), (2, one), (3, one)], [], [env["s", 2, three]])
    outputs = place([(0, two), (2, two), (3, two), (1, one), (1, two)], outputs, [env["s", 0, three]])
    spill_scores, primary, picked = place([(d, three) for d in (0, 1, 2, 3)], outputs, last_call=True)
    return (
        spill_scores.reshape(tile_dev * TILE, BLOCK),
        primary.reshape(tile_dev * TILE),
        picked.reshape(tile_dev * TILE),
    )


def solution(mesh):
    rows = P(AXES, None)
    flat = P(AXES)
    return jax.shard_map(
        functools.partial(local_part, 2),
        mesh=mesh,
        in_specs=(rows, flat, flat, flat, flat, P("region", "shard", None)),
        out_specs=(rows, flat, flat),
        check_vma=False,
    )
```

```python
import functools

import jax
import jax.numpy as jnp
from jax import lax
from jax.experimental import pallas as pl
from jax.experimental.pallas import tpu as pltpu
from jax.sharding import PartitionSpec as P

D = 768
TILE = 128
BLOCK = 512
SMALL_TERM = 1e-05
AXES = ("parts", "region", "shard")
F32 = jnp.float32
BF16 = jnp.bfloat16
I32 = jnp.int32
ANY = pl.BlockSpec(memory_space=pl.ANY)
SMEM = pl.BlockSpec(memory_space=pltpu.SMEM)
SHORT = pl.CostEstimate(flops=1, bytes_accessed=1, transcendentals=0)
VMEM_BYTES = 63 * 1024 * 1024 + 512 * 1024
VMEM_LESS = 60 * 1024 * 1024
VMEM = pl.BlockSpec(memory_space=pltpu.VMEM)


def ring_place(nz):
    ring = list(range(0, nz, 2))[:1] + list(range(1, nz, 2)) + list(range(2, nz, 2))[::-1]
    return ring, [ring.index(z) for z in range(nz)]


def place_of(z, nz):
    return jnp.where(z == 0, 0, jnp.where(z & 1 == 1, (z + 1) // 2, nz - z // 2))


def slot_of(nz, cap, blk_dev, at_ring, y, core, region, block):
    shard = block // blk_dev
    partner = 2 * ((shard & 1) ^ y) + (region ^ core)
    cls = lax.rem(at_ring - place_of(shard >> 1, nz) + nz, nz)
    at = partner * nz + cls
    return partner, cls * cap, at


def zero(ref, n):
    def body(i, carry):
        ref[i] = 0
        return carry

    lax.fori_loop(0, n, body, 0)


def plan_kernel(nz, cap, blk_dev, n_before, me, region, block, *refs):
    at_slot, inv, token, count = refs[n_before:]
    slots = nz * cap
    token[...] = jnp.zeros(token.shape, F32)

    def clear(i, carry):
        inv[i] = -1
        return carry

    lax.fori_loop(0, 4 * slots, clear, 0)
    zero(count, 4 * nz)

    def place(t, carry):
        partner, first, at = slot_of(nz, cap, blk_dev, me[0], me[1], me[2], region[t], block[t])
        rank = count[at]
        count[at] = rank + 1
        g = partner * slots + first + rank
        inv[g] = t
        at_slot[t] = g
        return carry

    lax.fori_loop(0, region.shape[0], place, 0)


def plan(me, region, block, before, nz, cap, blk_dev):
    return pl.pallas_call(
        functools.partial(plan_kernel, nz, cap, blk_dev, len(before)),
        out_shape=[
            jax.ShapeDtypeStruct(region.shape, I32),
            jax.ShapeDtypeStruct((4 * nz * cap,), I32),
            jax.ShapeDtypeStruct((8, TILE), F32),
        ],
        in_specs=[SMEM, SMEM, SMEM] + [ANY] * len(before),
        out_specs=[SMEM, SMEM, VMEM],
        scratch_shapes=[pltpu.SMEM((4 * nz,), I32)],
        compiler_params=pltpu.CompilerParams(vmem_limit_bytes=VMEM_BYTES),
        cost_estimate=SHORT,
        name="plan",
    )(me, region, block, *before)


def receive_kernel(nz, cap, blk_dev, tile_dev, me, *refs):
    packs, (meta, ids, held, scalars, count, held_sems, scalar_sems) = refs[:4], refs[4:]
    slots = nz * cap
    at_ring, y, core = me[0], me[1], me[2]

    def copies(d):
        return (
            pltpu.make_async_copy(packs[d], held.at[d], held_sems.at[d]),
            pltpu.make_async_copy(packs[d].at[pl.ds(2 * tile_dev, 8)], scalars.at[d], scalar_sems.at[d]),
        )

    for d in range(4):
        for copy in copies(d):
            copy.start()

    def clear(i, carry):
        ids[i] = -1
        return carry

    lax.fori_loop(0, 4 * slots, clear, 0)
    for d in range(4):
        for copy in copies(d):
            copy.wait()
        zero(count, 4 * nz)

        def place(t, carry):
            block = scalars[d, 1, t]
            partner, first, at = slot_of(
                nz, cap, blk_dev, at_ring, y ^ (d >> 1), core ^ (d & 1), scalars[d, 0, t], block
            )

            @pl.when(partner == d)
            def _():
                rank = count[at]
                count[at] = rank + 1
                g = d * slots + first + rank
                ids[g] = lax.rem(block, blk_dev)
                meta[g, 1:2, :] = held[d, pl.ds(t, 1), :]
                meta[g, 2:3, :] = held[d, pl.ds(tile_dev + t, 1), :]

            return carry

        lax.fori_loop(0, tile_dev, place, 0)


def receive(me, packs, nz, cap, blk_dev, tile_dev):
    slots = nz * cap
    return pl.pallas_call(
        functools.partial(receive_kernel, nz, cap, blk_dev, tile_dev),
        out_shape=[
            jax.ShapeDtypeStruct((4 * slots, 8, TILE), I32),
            jax.ShapeDtypeStruct((4 * slots,), I32),
        ],
        in_specs=[SMEM] + [ANY] * 4,
        out_specs=[VMEM, SMEM],
        scratch_shapes=[
            pltpu.VMEM((4,) + packs[0].shape, I32),
            pltpu.SMEM((4, 8, TILE), I32),
            pltpu.SMEM((4 * nz,), I32),
            pltpu.SemaphoreType.DMA((4,)),
            pltpu.SemaphoreType.DMA((4,)),
        ],
        compiler_params=pltpu.CompilerParams(vmem_limit_bytes=VMEM_BYTES),
        cost_estimate=SHORT,
        name="receive",
    )(me, *packs)


def dispatch_kernel(slots, runs, n_before, at_slot, vec, *refs):
    refs = refs[n_before:]
    tiles, (held, in_sems, out_sems) = refs[: len(runs)], refs[len(runs) :]
    tile_dev = vec.shape[0]

    def each(act):
        def body(t, carry):
            g = at_slot[t]

            @pl.when(g >= slots)
            def _():
                act(t, g)

            return carry

        lax.fori_loop(0, tile_dev, body, 0)

    def bring(t, g):
        pltpu.make_async_copy(vec.at[t], held.at[t], in_sems.at[t]).start()

    def send(t, g):
        pltpu.make_async_copy(vec.at[t], held.at[t], in_sems.at[t]).wait()
        for ref, (d, first, count) in zip(tiles, runs):
            begin = d * slots + first

            @pl.when((g >= begin) & (g < begin + count))
            def _():
                pltpu.make_async_copy(held.at[t], ref.at[g - begin], out_sems.at[t]).start()

    def finish(t, g):
        pltpu.make_async_copy(held.at[t], tiles[0].at[0], out_sems.at[t]).wait()

    each(bring)
    each(send)
    each(finish)


def dispatch(at_slot, vec, before, slots, runs):
    tile_dev = vec.shape[0]
    return pl.pallas_call(
        functools.partial(dispatch_kernel, slots, runs, len(before)),
        out_shape=[jax.ShapeDtypeStruct((count, TILE, D), BF16) for _, _, count in runs],
        in_specs=[SMEM, ANY] + [ANY] * len(before),
        out_specs=[ANY] * len(runs),
        scratch_shapes=[
            pltpu.VMEM((tile_dev, TILE, D), BF16),
            pltpu.SemaphoreType.DMA((tile_dev,)),
            pltpu.SemaphoreType.DMA((tile_dev,)),
        ],
        compiler_params=pltpu.CompilerParams(vmem_limit_bytes=VMEM_BYTES),
        cost_estimate=SHORT,
        name="dispatch",
    )(at_slot, vec, *before)


def gate_kernel(*refs):
    pass


def gate(passed, others=()):
    n = len(passed)
    return pl.pallas_call(
        gate_kernel,
        out_shape=[jax.ShapeDtypeStruct(v.shape, v.dtype) for v in passed],
        in_specs=[ANY] * (n + len(others)),
        out_specs=[ANY] * n,
        input_output_aliases={i: i for i in range(n)},
        compiler_params=pltpu.CompilerParams(vmem_limit_bytes=VMEM_BYTES),
        cost_estimate=SHORT,
        name="gate",
    )(*passed, *others)


def score_math(points, block_rows, meta):
    picks = meta.astype(F32).T.astype(I32)
    lane = lax.broadcasted_iota(I32, (TILE, BLOCK), 1)
    onehot = (lane == picks[:, 1:2]).astype(F32).astype(BF16)
    chosen = jnp.dot(onehot, block_rows, preferred_element_type=F32)
    point_f = points.astype(F32)
    residue = point_f - chosen
    point_sq = jnp.sum(point_f * point_f, axis=1, keepdims=True)
    residue_sq = jnp.sum(residue * residue, axis=1, keepdims=True)
    along = jnp.sum(residue * point_f, axis=1, keepdims=True)
    both = jnp.concatenate([points, residue.astype(BF16)], axis=0)
    products = lax.dot_general(
        both, block_rows, (((1,), (1,)), ((), ())), preferred_element_type=F32
    )
    cross, against = products[:TILE], products[TILE:]
    block_f = block_rows.astype(F32)
    squares = block_f * block_f
    partial = squares[:, :128]
    for k in range(1, D // 128):
        partial = partial + squares[:, k * 128 : (k + 1) * 128]
    center_sq = jnp.sum(partial.T, axis=0, keepdims=True)
    distance = point_sq - 2.0 * cross + center_sq
    mean_sq = residue_sq / D
    off = (along - against) / D
    scores = (distance / D + off * off * (1.0 / (mean_sq + SMALL_TERM))).astype(BF16)
    picked = jnp.sum(
        jnp.where(lane == picks[:, 2:3], scores.astype(F32), 0.0), axis=1, keepdims=True
    )
    column = lax.broadcasted_iota(I32, (TILE, 128), 1)
    small = jnp.where(column == 0, mean_sq, jnp.where(column == 1, picked, 0.0))
    return scores, small.T[:8]


def score_kernel(nz, cap, blk_dev, places, wide, runs, fetched, late, resident, aliased, n_extra, me, ids, inv, meta, *refs):
    slots = nz * cap
    n = len(places)
    tiles, refs = refs[: len(runs)], refs[len(runs) :]
    local, parts = refs[0], refs[1 : 1 + len(fetched)]
    refs = refs[1 + len(fetched) + aliased + n_extra :]
    scores = refs[:n]
    work, xbuf, cbuf, obuf, tail, tail_b, xsem, csem, osem, tsem = refs[n:]
    half = me[3]
    half_blocks = blk_dev // 2

    total = jnp.int32(0)
    for place, (partner, base) in enumerate(places):
        for k in range(wide):
            b = ids[partner * slots + base + k]
            valid = b >= 0
            if late is not None:
                first, wanted = late
                is_late = (b // half_blocks != half) & (b % half_blocks >= first)
                is_late = is_late & ((base + k) // cap == nz - 1)
                valid = valid & (is_late == wanted)
            work[total] = place * wide + k
            total = total + valid.astype(I32)

    def where(i):
        code = work[i]
        place = code // wide
        partner, base = jnp.int32(places[0][0]), jnp.int32(places[0][1])
        for other in range(1, n):
            partner = jnp.where(place == other, places[other][0], partner)
            base = jnp.where(place == other, places[other][1], base)
        k = code - place * wide
        return place, k, partner, base + k

    def start(i):
        place, k, partner, slot = where(i)
        b = ids[partner * slots + slot]
        for ref, (d, first, count) in zip(tiles, runs):
            row = slot - first if d else jnp.maximum(inv[slot], 0)

            @pl.when((partner == d) & (slot >= first) & (slot < first + count))
            def _():
                pltpu.make_async_copy(ref.at[row], xbuf.at[i], xsem.at[i]).start()

        cls = slot // cap
        own = b // half_blocks == half
        inside = b % half_blocks

        if resident:
            return

        if any(base == 0 for _, base in places):

            @pl.when(cls == 0)
            def _():
                pltpu.make_async_copy(local.at[b], cbuf.at[i], csem.at[i]).start()

        for ref, (hops, direct, first, count) in zip(parts, fetched):
            right = own if direct else jnp.logical_not(own)

            @pl.when((cls == hops) & right & (inside >= first) & (inside < first + count))
            def _():
                rows = ref.at[inside - first, pl.ds(0, BLOCK)]
                pltpu.make_async_copy(rows, cbuf.at[i], csem.at[i]).start()

    def begin(i, carry):
        start(i)
        return carry

    def whole_parts():
        at = 0
        for p, (ref, (hops, direct, first, count)) in enumerate(zip(parts, fetched)):
            yield pltpu.make_async_copy(ref, cbuf.at[pl.ds(at, count)], csem.at[p])
            at += count

    if resident:
        for copy in whole_parts():
            copy.start()
    lax.fori_loop(0, total, begin, 0)
    tail_rows = pl.ds(wide * TILE + 16 * (aliased > 0), 16)
    tail[...] = jnp.zeros(tail.shape, F32)

    def centers_of(i, slot, partner):
        if not resident:
            return cbuf[i]
        inside = ids[partner * slots + slot] % half_blocks
        row, at = jnp.int32(0), 0
        for hops, direct, first, count in fetched:
            row = jnp.where((inside >= first) & (inside < first + count), at + inside - first, row)
            at += count
        return cbuf[row]

    def body(pair, carry):
        both = (2 * pair, jnp.minimum(2 * pair + 1, total - 1))
        spots = [where(i) for i in both]
        values = []
        for j, i in enumerate(both):

            @pl.when(2 * pair + j < total)
            def _():
                pltpu.make_async_copy(tiles[0].at[0], xbuf.at[i], xsem.at[i]).wait()
                if not resident:
                    pltpu.make_async_copy(local.at[0], cbuf.at[i], csem.at[i]).wait()

        for i, (place, k, partner, slot) in zip(both, spots):
            rows = centers_of(i, slot, partner)
            values.append(score_math(xbuf[i], rows, meta[partner * slots + slot]))
        for i, (place, k, _, _), (value, rows) in zip(both, spots, values):
            obuf[i] = value
            tail[place, pl.ds(k, 1), 0 : 2 * TILE] = jnp.concatenate([rows[0:1], rows[1:2]], axis=1)
        for j, (i, (place, k, _, _)) in enumerate(zip(both, spots)):
            for other in range(n):

                @pl.when((place == other) & (2 * pair + j < total))
                def _():
                    pltpu.make_async_copy(
                        obuf.at[i], scores[other].at[pl.ds(k * TILE, TILE)], osem.at[i]
                    ).start()

        return carry

    if resident:
        for copy in whole_parts():
            copy.wait()
    lax.fori_loop(0, (total + 1) // 2, body, 0)

    tail_b[...] = tail[...].astype(BF16)
    for place in range(n):
        pltpu.make_async_copy(tail_b.at[place], scores[place].at[tail_rows], tsem.at[place]).start()

    def finish(i, carry):
        pltpu.make_async_copy(obuf.at[i], scores[0].at[pl.ds(0, TILE)], osem.at[i]).wait()
        return carry

    lax.fori_loop(0, total, finish, 0)
    for place in range(n):
        pltpu.make_async_copy(tail_b.at[place], scores[place].at[tail_rows], tsem.at[place]).wait()


def score_call(
    nz, cap, blk_dev, places, wide, runs, fetched, late, resident, me, ids, inv, meta, tiles, local, parts, before, extra
):
    n = len(places)
    items = n * wide
    first_before = 5 + len(runs) + len(parts)
    return pl.pallas_call(
        functools.partial(
            score_kernel, nz, cap, blk_dev, places, wide, runs, fetched, late, resident, len(before), len(extra)
        ),
        out_shape=[
            jax.ShapeDtypeStruct((wide * TILE + ((48 if d == 2 else 32) if late else 16), BLOCK), BF16) for d, _ in places
        ],
        in_specs=[SMEM, SMEM, SMEM, VMEM]
        + [ANY] * (len(runs) + 1)
        + [ANY] * (len(parts) + len(before) + len(extra)),
        out_specs=[ANY] * n,
        scratch_shapes=[
            pltpu.SMEM((items + 1,), I32),
            pltpu.VMEM((items, TILE, D), BF16),
            pltpu.VMEM((sum(key[3] for key in fetched) if resident else items, BLOCK, D), BF16),
            pltpu.VMEM((items, TILE, BLOCK), BF16),
            pltpu.VMEM((n, 16, BLOCK), F32),
            pltpu.VMEM((n, 16, BLOCK), BF16),
            pltpu.SemaphoreType.DMA((items,)),
            pltpu.SemaphoreType.DMA((items,)),
            pltpu.SemaphoreType.DMA((items,)),
            pltpu.SemaphoreType.DMA((n,)),
        ],
        input_output_aliases={first_before + i: i for i in range(len(before))},
        compiler_params=pltpu.CompilerParams(vmem_limit_bytes=VMEM_BYTES),
        cost_estimate=SHORT,
        name="score",
    )(me, ids, inv, meta, *tiles, local, *parts, *before, *extra)


def assemble_kernel(spans, held_already, n_before, n_earlier, last, inv, *refs):
    n = len(spans)
    sources, before, refs = refs[:n], refs[n : n + n_before], refs[n + n_before + n_earlier :]
    out, primary_out, picked_out, primary, picked, held, tail, in_sems, out_sems, tail_sems = refs
    if n_before:
        primary[...] = before[1][...]
        picked[...] = before[2][...]

    def each(act):
        at = 0
        for d, (first, wide) in enumerate(spans):
            for k in range(wide):
                t = inv[first + k]

                @pl.when(t >= 0)
                def _():
                    act(d, pl.ds(k * TILE, TILE), t, at, k)

                at += 1

    def tail_rows(d):
        return min(32, sources[d].shape[0] - spans[d][1] * TILE)

    def tail_copy(d):
        return pltpu.make_async_copy(
            sources[d].at[pl.ds(spans[d][1] * TILE, tail_rows(d))], tail.at[d, pl.ds(0, tail_rows(d))], tail_sems.at[d]
        )

    def bring(d, rows, t, at, k):
        if not held_already[d]:
            pltpu.make_async_copy(sources[d].at[rows], held.at[at], in_sems.at[at]).start()

    def send(d, rows, t, at, k):
        if held_already[d]:
            pltpu.make_async_copy(sources[d].at[rows], out.at[t], out_sems.at[at]).start()
        else:
            pltpu.make_async_copy(sources[d].at[rows], held.at[at], in_sems.at[at]).wait()
            pltpu.make_async_copy(held.at[at], out.at[t], out_sems.at[at]).start()

    def finish(d, rows, t, at, k):
        pltpu.make_async_copy(held.at[at], out.at[t], out_sems.at[at]).wait()

    for d in range(n):
        if not held_already[d]:
            tail_copy(d).start()
    each(bring)
    each(send)
    values = []
    for d in range(n):
        if held_already[d]:
            both = sources[d][pl.ds(spans[d][1] * TILE, tail_rows(d))].astype(F32)
        else:
            tail_copy(d).wait()
            both = tail[d, pl.ds(0, tail_rows(d))].astype(F32)
        values.append(both if both.shape[0] == 16 else both[:16] + both[16:])

    def write(d, rows, t, at, k):
        primary[pl.ds(t, 1), :] = values[d][k : k + 1, :TILE]
        picked[pl.ds(t, 1), :] = values[d][k : k + 1, TILE : 2 * TILE]

    each(write)
    primary_out[...] = primary[...].astype(primary_out.dtype)
    picked_out[...] = picked[...].astype(picked_out.dtype)
    each(finish)


def assemble(tile_dev, spans, inv, sources, before, earlier, last):
    n = len(sources)
    count = sum(wide for _, wide in spans)
    tail_rows = 32 if last else 16
    held_already = [last and i > 0 for i in range(n)]
    return pl.pallas_call(
        functools.partial(assemble_kernel, spans, held_already, len(before), len(earlier), last),
        out_shape=[jax.ShapeDtypeStruct((tile_dev, TILE, BLOCK), BF16)]
        + [jax.ShapeDtypeStruct((tile_dev, TILE), BF16 if last else F32)] * 2,
        in_specs=[SMEM]
        + [VMEM if held else ANY for held in held_already]
        + [ANY, VMEM, VMEM][: len(before)]
        + [ANY] * len(earlier),
        out_specs=[ANY, VMEM, VMEM],
        scratch_shapes=[
            pltpu.VMEM((tile_dev, TILE), F32),
            pltpu.VMEM((tile_dev, TILE), F32),
            pltpu.VMEM((count, TILE, BLOCK), BF16),
            pltpu.VMEM((n, tail_rows, BLOCK), BF16),
            pltpu.SemaphoreType.DMA((count,)),
            pltpu.SemaphoreType.DMA((count,)),
            pltpu.SemaphoreType.DMA((n,)),
        ],
        input_output_aliases={1 + n: 0} if before else {},
        compiler_params=pltpu.CompilerParams(vmem_limit_bytes=VMEM_LESS if last else VMEM_BYTES),
        cost_estimate=SHORT,
        name="assemble",
    )(inv, *sources, *before, *earlier)


def cut_kernel(first, source, target, held, in_sems, out_sems):
    step = BLOCK // 4
    runs = [(i, pl.ds(j * step, step)) for i in range(target.shape[0]) for j in range(4)]
    brought = [
        pltpu.make_async_copy(source.at[first + i, rows], held.at[i, rows], in_sems.at[n])
        for n, (i, rows) in enumerate(runs)
    ]
    sent = [
        pltpu.make_async_copy(held.at[i, rows], target.at[i, rows], out_sems.at[n])
        for n, (i, rows) in enumerate(runs)
    ]
    for copy in brought:
        copy.start()
    for arrived, copy in zip(brought, sent):
        arrived.wait()
        copy.start()
    for copy in sent:
        copy.wait()


def own_kernel(blocks, source, *refs):
    pieces, (held, in_sems, out_sems) = refs[:-3], refs[-3:]
    total = blocks * len(pieces)
    first = (lax.axis_index("parts") & 1) * total
    brought = [
        pltpu.make_async_copy(source.at[first + i], held.at[i], in_sems.at[i]) for i in range(total)
    ]
    sent = [
        pltpu.make_async_copy(held.at[i], pieces[i // blocks].at[i % blocks], out_sems.at[i]) for i in range(total)
    ]
    for copy in brought:
        copy.start()
    for arrived, copy in zip(brought, sent):
        arrived.wait()
        copy.start()
    for copy in sent:
        copy.wait()


def own_pieces(source, pieces, blocks):
    total = pieces * blocks
    return pl.pallas_call(
        functools.partial(own_kernel, blocks),
        out_shape=[jax.ShapeDtypeStruct((blocks, BLOCK, D), BF16)] * pieces,
        in_specs=[ANY],
        out_specs=[ANY] * pieces,
        scratch_shapes=[
            pltpu.VMEM((total, BLOCK, D), BF16),
            pltpu.SemaphoreType.DMA((total,)),
            pltpu.SemaphoreType.DMA((total,)),
        ],
        compiler_params=pltpu.CompilerParams(vmem_limit_bytes=VMEM_BYTES),
        cost_estimate=SHORT,
        name="own_pieces",
    )(source)


def cut(source, first, count, rows=BLOCK):
    return pl.pallas_call(
        functools.partial(cut_kernel, first),
        out_shape=jax.ShapeDtypeStruct((count, rows, D), BF16),
        in_specs=[ANY],
        out_specs=ANY,
        scratch_shapes=[
            pltpu.VMEM((count, BLOCK, D), BF16),
            pltpu.SemaphoreType.DMA((4 * count,)),
            pltpu.SemaphoreType.DMA((4 * count,)),
        ],
        compiler_params=pltpu.CompilerParams(vmem_limit_bytes=VMEM_BYTES),
        cost_estimate=SHORT,
        name="cut",
    )(source)


def local_part(pieces, vectors, tile_region, tile_block, primary_pick, spill_pick, centers):
    n_parts, n_region, n_shard = (lax.axis_size(a) for a in AXES)
    nz = n_shard // 2
    tile_dev = tile_region.shape[0]
    cap = 2 * tile_dev // (n_region * n_shard)
    slots = nz * cap
    blk_dev = centers.shape[1] // BLOCK
    half_blocks = blk_dev // 2
    pieces = min(pieces, half_blocks)
    sub_blocks = half_blocks // pieces
    shard = lax.axis_index("shard")
    half = lax.axis_index("parts") & 1
    ring, at_ring = ring_place(nz)
    me = jnp.stack(
        [place_of(shard >> 1, nz), shard & 1, lax.axis_index("region"), half]
    ).astype(I32)

    def device(p, r, s):
        return (p * n_region + r) * n_shard + s

    every = [(p, r, s) for p in range(n_parts) for r in range(n_region) for s in range(n_shard)]

    def permute(value, target):
        return lax.ppermute(value, AXES, [(device(*a), device(*target(*a))) for a in every])

    def next_z(p, r, s):
        return (p, r, 2 * ring[(at_ring[s >> 1] + 1) % nz] + (s & 1))

    def other_part(p, r, s):
        return (p ^ 1, r, s)

    local = centers[0].reshape(blk_dev, BLOCK, D)

    own = own_pieces(local, pieces, sub_blocks)
    tile_rows = vectors.reshape(tile_dev, TILE, D)
    scalars = jnp.pad(jnp.stack([tile_region, tile_block]), ((0, 6), (0, TILE - tile_dev)))
    pack = jnp.concatenate(
        [primary_pick.reshape(tile_dev, TILE), spill_pick.reshape(tile_dev, TILE), scalars]
    )
    at_slot, inv, token = plan(me, tile_region, tile_block, own, nz, cap, blk_dev)

    def exchange(value, partner):
        if partner == 0:
            return value
        return permute(value, lambda p, r, s: (p, r ^ (partner & 1), s ^ (partner >> 1)))

    packs = [exchange(pack, d) for d in range(4)]
    part = slots // 2
    runs = tuple((d, first, part) for first in (0, part) for d in (2, 3, 1))
    sent = dispatch(at_slot, tile_rows, packs[1:], slots, runs)
    meta, ids = receive(me, packs, nz, cap, blk_dev, tile_dev)

    env, waits, opens = {}, {}, {}

    def across(d):
        return lambda p, r, s: (p, r ^ (d & 1), s ^ (d >> 1))

    steps = (nz - 1) * pieces
    split = sub_blocks // 2 if nz > 2 else 0
    last = steps + 1
    fetched = {}
    starts = {}
    env.update({("z", i + 1 - pieces): own[i] for i in range(pieces)})

    def start(at, name, payload, target, done):
        starts.setdefault(at, []).append((name, payload, target, done))

    for k in range(1, steps + 1):
        hops, first = (k - 1) // pieces + 1, (k - 1) % pieces * sub_blocks
        if split and k == steps:
            start(k - 2, ("z", k), "wide", next_z, None)
            start(k - 1, ("z", last), ("cut", 0), next_z, None)
            fetched[hops, True, first, sub_blocks] = ("z", k)
            fetched[hops, False, first, split] = ("x", k)
            fetched[hops, False, first + split, sub_blocks - split] = ("z", last)
        else:
            start(max(0, k - 2), ("z", k), ("z", k - pieces), next_z, k)
            start(k, ("x", k), ("z", k), other_part, k + 1 if k < steps else None)
            fetched[hops, True, first, sub_blocks] = ("z", k)
            fetched[hops, False, first, sub_blocks] = ("x", k)

    times = {0: (0, 2), 1: (0, 3), 2: (5, 6), 3: (2, 4), 4: (3, 5), 5: (5, 6)}
    for i, run in enumerate(runs):
        if run[0] == 1:
            continue
        at, done = (min(g, last - 2 + j) for j, g in enumerate(times[i]))
        env["sent", i] = sent[i]
        if at:
            opens.setdefault(at, []).append(("sent", i))
        start(at, ("t", i), ("sent", i), across(run[0]), done)
    for i, run in enumerate(runs):
        if run[0] == 1:
            env["sent", i] = sent[i]
            at = last if run[1] else min(5, last - 1)
            opens.setdefault(at, []).append(("sent", i))
            start(at, ("t", i), ("sent", i), across(1), None)
    env["t", len(runs)] = tile_rows
    runs += ((0, 0, slots),)

    def score(where, late=None, into=False, extra=()):
        resident = into
        keys = tuple(
            key
            for key in fetched
            if any(key[0] in group for _, group in where)
            and (late is None or (fetched[key] in (("x", steps), ("z", last))) == resident)
        )
        wide = len(where[0][1]) * cap
        places = tuple((d, group[0] * cap) for d, group in where)
        used = [
            i
            for i, (d, first, count) in enumerate(runs)
            if any(d == partner and first < base + wide and first + count > base for partner, base in places)
        ]
        scores = score_call(
            nz, cap, blk_dev, places, wide, tuple(runs[i] for i in used), keys, late, resident, me, ids, inv, meta,
            [env["t", i] for i in used], local,
            [env[fetched[key]] for key in keys],
            [env["s", d, group] for d, group in where] if into else [],
            extra,
        )
        for (d, group), values in zip(where, scores):
            env["s", d, group] = values

    def place(sources, before, earlier=(), last_call=False):
        return assemble(
            tile_dev,
            [(d * slots + group[0] * cap, len(group) * cap) for d, group in sources],
            inv,
            [env["r" if d else "s", d, group] for d, group in sources],
            before,
            earlier,
            last_call,
        )

    one, two, three = (tuple(range(a, b)) for a, b in ((0, nz // 2), (nz // 2, 3 * nz // 4), (3 * nz // 4, nz)))
    plans, at_once = {}, {}
    for ready, order, group, back in (
        (3, (2, 3, 0), one, {2: (4, 5), 3: (5, 6)}),
        (5, (2, 3, 0), two, {2: (0, 6), 3: (6, 7)}),
        (5, (1,), one, {}),
    ):
        ready = max(ready, group[-1] * pieces + 1)
        plans.setdefault(ready, []).append((group, order))
        for d, (at, done) in back.items():
            if at:
                at = min(last - 1, max(at, ready + 1))
                opens.setdefault(at, []).append(("s", d, group))
                start(at, ("r", d, group), ("s", d, group), across(d), min(last, max(done, at + 1)))
            else:
                at_once.setdefault(ready, []).append((d, group, min(last, max(done, ready + 1))))
    opens.setdefault(last - 1, []).append(("s", 1, one))
    first_late = (pieces - 1) * sub_blocks
    env["token"] = token
    for k in range(last + 1):
        if k:
            passed = waits.get(k, []) + opens.get(k, [])
            source = ("z", k + 2 - pieces)
            if k + 2 <= steps and k + 2 - pieces < k:
                passed.append(source)
            passed.append("token")
            others = [env["x", steps], env["z", last]] if split and k == last else []
            for name, value in zip(passed, gate([env[n] for n in passed], others)):
                env[name] = value
        if split and k == steps - 2:
            env["wide"] = cut(env["z", k], 0, sub_blocks, rows=BLOCK + 16)
        if split and k == steps - 1:
            env["cut", 0] = cut(env["x", steps - pieces], split, sub_blocks - split)
        for name, payload, target, done in starts.get(k, []):
            env[name] = permute(env[payload], target)
            if done is not None:
                waits.setdefault(done, []).append(name)
        for group, order in plans.get(k, []):
            score([(d, group) for d in order], extra=[env["token"]])
        if split and k == steps - 1:
            env["x", steps] = permute(cut(env["z", steps], 0, split), other_part)
        for d, group, done in at_once.get(k, []):
            env["r", d, group] = exchange(env["s", d, group], d)
            waits.setdefault(done, []).append(("r", d, group))
        if k == last - 1:
            score([(d, three) for d in (2, 3)], (first_late, False), extra=[env["token"]])
    for d in (2, 3):
        score([(d, three)], (first_late, True), True, [env["token"] if d == 2 else env["s", 2, three]])
        env["r", d, three] = exchange(env["s", d, three], d)
    score([(1, two), (1, three), (0, three)], extra=[env["s", 3, three]])
    for group in (one, two, three):
        env["r", 1, group] = exchange(env["s", 1, group], 1)
    outputs = place([(0, one), (2, one), (3, one)], [], [env["s", 2, three]])
    outputs = place([(0, two), (2, two), (3, two), (1, one), (1, two)], outputs, [env["s", 0, three]])
    spill_scores, primary, picked = place([(d, three) for d in (0, 1, 2, 3)], outputs, last_call=True)
    return (
        spill_scores.reshape(tile_dev * TILE, BLOCK),
        primary.reshape(tile_dev * TILE),
        picked.reshape(tile_dev * TILE),
    )


def solution(mesh):
    rows = P(AXES, None)
    flat = P(AXES)
    return jax.shard_map(
        functools.partial(local_part, 2),
        mesh=mesh,
        in_specs=(rows, flat, flat, flat, flat, P("region", "shard", None)),
        out_specs=(rows, flat, flat),
        check_vma=False,
    )
```
